256 devices in a mesh: dp: 32 (over y_hi, z, core), tensor: 8 (over y_lo, x).
Axes of the slice: x: 4, y: 4 (y_hi: 2, y_lo: 2; y = y_hi * 2 + y_lo), z: 8, core: 2. Of those that a mesh axis runs over, the one named last changes fastest.
Arguments:
- activations: bfloat16 [2, 8192, 14848], P(None, 'dp', 'tensor'), may hold values from -6 to 6
- cotangent: bfloat16 [2, 8192, 14848], P(None, 'dp', 'tensor'), may hold values from -6 to 6
- rewards: float32 [64], P('dp'), may hold values from -6 to 6
- group_of: int32 [64], P('dp'), may hold values from 0 to 15
- layer_owner: int32 [2], replicated, may hold values from 0 to 31
- adapter_a: bfloat16 [32, 2, 64, 14848], P('dp', None, None, 'tensor'), may hold values from -6 to 6
- adapter_b: bfloat16 [32, 2, 64, 14848], P('dp', None, None, 'tensor'), may hold values from -6 to 6
- frozen_query_part: bfloat16 [2, 2, 2048, 14848], P(None, None, 'dp', 'tensor'), may hold values from -32 to 32
- decode_in: bfloat16 [2, 2, 2048, 14848], P(None, None, 'dp', 'tensor'), may hold values from -6 to 6
- kv_cache: bfloat16 [2, 2048, 8, 96, 128], P(None, 'dp', 'tensor'), may hold values from -32 to 32
- new_kv: bfloat16 [2, 2, 2048, 8, 128], P(None, None, 'dp', 'tensor'), may hold values from -6 to 6
- lengths: int32 [2048], P('dp'), may hold values from 2 to 96, as said below
Outputs:
- new_a: bfloat16 [2, 64, 14848], P(None, None, 'tensor')
- revised_up_factors: bfloat16 [2, 64, 14848], P(None, None, 'tensor')
- attended: bfloat16 [2, 2, 2048, 14848], P(None, None, 'dp', 'tensor')
The draws below stay inside these ranges and needn't reach their ends.
Inputs may be any that keep to these rules, and one draw needn't show every extreme that they name: `layer_owner`: index along dp of the replica whose copy of layer l's adapter is current. `lengths`: in each aligned block of 64 rows some row has all 96 slots valid.
All inputs are finite; a program needn't handle non-finite values.
Results may differ from the reference program's by a relative error of at most 0.02525.
Values may be sent and summed in bfloat16 or wider, within the bound.
No kernel may reach another device: no remote copies, remote signals or barrier semaphores. Data moves between devices by JAX's collectives and lax.ppermute only.
A program may use at most 64 MiB of HBM per device.

```python
import math
import jax
import jax.numpy as jnp
from jax import lax

D = 14848
HEADS = 232
KVH = 8
HD = 64
R = 64
L = 2
STEPS = 2
SEQ_LEN = 128
ROWS_DEV = 64
CTX = 96
TOKENS = 8192
COMPL = 64
GROUPS = 16
ROWS = 2048
COPIES = 32
N_DP = 32


def draw_kv_cache(key, part):
    key = jax.random.fold_in(key, 3)
    filled = jax.random.normal(key, (L, ROWS, KVH, CTX, 2 * HD), jnp.float32)
    return filled.astype(jnp.bfloat16)


def draw_frozen_query_part(key, part):
    key = jax.random.fold_in(key, 5)
    result = jax.random.normal(key, (STEPS, L, ROWS, D), jnp.float32)
    return result.astype(jnp.bfloat16)


def draw_lengths(key, part):
    key = jax.random.fold_in(key, 7)
    length_key, place_key = jax.random.split(key)
    drawn = jax.random.randint(length_key, (ROWS,), 2, CTX + 1)
    blocks = ROWS // ROWS_DEV
    chosen = jax.random.randint(place_key, (blocks,), 0, ROWS_DEV)
    within = jnp.arange(ROWS, dtype=jnp.int32) % ROWS_DEV
    target = jnp.repeat(chosen, ROWS_DEV)
    return jnp.where(within == target, CTX, drawn).astype(jnp.int32)


def set_ends(values, stream_key, smallest, high):
    spot = [jax.random.randint(jax.random.fold_in(stream_key, axis), (), 0, length) for axis, length in enumerate(values.shape)]
    widest = values.shape.index(max(values.shape))
    next_to = spot[:widest] + [(spot[widest] + 1) % values.shape[widest]] + spot[widest + 1:]
    return values.at[tuple(spot)].set(smallest).at[tuple(next_to)].set(high)


def shard_levels(stream_key, shape, shards, low, high):
    loudness = 1.0
    for position, parts in shards:
        draws = jax.random.uniform(jax.random.fold_in(jax.random.fold_in(stream_key, 6), position), (parts,), jnp.float32, low / len(shards), high / len(shards))
        loudness = loudness * jnp.repeat(jnp.exp(draws), shape[position] // parts).reshape((-1,) + (1,) * (len(shape) - 1 - position))
    return loudness


def centred(stream_key, shape, width, limit, pieces=(), held_as=jnp.bfloat16):
    values = width * jax.random.normal(stream_key, shape, jnp.float32)
    if pieces:
        values = values * shard_levels(stream_key, shape, pieces, -0.22, 0.18)
    return jnp.clip(values, -limit, limit).astype(held_as)


def setup_inputs(seed: int = 0) -> dict:
    streams_of = jax.random.split(jax.random.key(seed), 13)
    return {
        "activations": centred(streams_of[0], (L, TOKENS, D), 1.0, 6.0, ((1, 32), (2, 8))),
        "cotangent": centred(streams_of[1], (L, TOKENS, D), 1.0, 6.0, ((1, 32), (2, 8))),
        "rewards": centred(streams_of[2], (COMPL,), 1.0, 6.0, ((0, 32),), jnp.float32),
        "group_of": set_ends(jax.random.randint(streams_of[3], (COMPL,), 0, GROUPS), jax.random.fold_in(streams_of[3], 1), 0, GROUPS - 1).astype(jnp.int32),
        "layer_owner": jax.random.randint(streams_of[4], (L,), 0, N_DP).astype(jnp.int32),
        "adapter_a": centred(streams_of[5], (COPIES, L, R, D), 1.0, 6.0, ((0, 32), (3, 8))),
        "adapter_b": centred(streams_of[6], (COPIES, L, R, D), 1.0, 6.0, ((0, 32), (3, 8))),
        "frozen_query_part": draw_frozen_query_part(jax.random.fold_in(streams_of[12], 71), 0),
        "decode_in": centred(streams_of[8], (STEPS, L, ROWS, D), 1.0, 6.0, ((2, 32), (3, 8))),
        "kv_cache": draw_kv_cache(jax.random.fold_in(streams_of[12], 71), 0),
        "new_kv": centred(streams_of[10], (STEPS, L, ROWS, KVH, 2 * HD), 1.0, 6.0, ((2, 32), (3, 8))),
        "lengths": draw_lengths(jax.random.fold_in(streams_of[12], 71), 0),
    }


rate_a = 0.5
rate_b = 0.05

def advantage_of(rewards, group_of):
    labels = jnp.arange(GROUPS, dtype=jnp.int32)
    member = (group_of[:, None] == labels[None, :]).astype(jnp.float32)
    group_sum = lax.optimization_barrier(jnp.sum(member * rewards[:, None], axis=0))
    group_count = lax.optimization_barrier(jnp.sum(member, axis=0))
    group_mean = group_sum / jnp.maximum(group_count, 1.0)
    return rewards - lax.optimization_barrier(jnp.sum(member * group_mean[None, :], axis=1))

def reference(activations, cotangent, rewards, group_of, layer_owner, adapter_a, adapter_b, frozen_query_part, decode_in, kv_cache, new_kv, lengths):
    scale_a = D ** (-0.5)
    up_factor_scale = R ** (-0.5)
    advantage = advantage_of(rewards, group_of)
    tok_adv = jnp.repeat(advantage, SEQ_LEN)
    updated_a = []
    updated_b = []
    for layer_index in range(L):
        factor_a = adapter_a[layer_owner[layer_index], layer_index]
        factor_b = adapter_b[layer_owner[layer_index], layer_index]
        inputs = activations[layer_index]
        weighted = (tok_adv[:, None] * cotangent[layer_index].astype(jnp.float32)).astype(jnp.bfloat16)
        low_rank = (jnp.dot(inputs, factor_a.T, preferred_element_type=jnp.float32) * scale_a).astype(jnp.bfloat16)
        back_rank = (jnp.dot(weighted, factor_b.T, preferred_element_type=jnp.float32) * up_factor_scale).astype(jnp.bfloat16)
        grad_a = jnp.dot(back_rank.T, inputs, preferred_element_type=jnp.float32) * scale_a
        grad_b = jnp.dot(low_rank.T, weighted, preferred_element_type=jnp.float32) * up_factor_scale
        updated_a.append((factor_a.astype(jnp.float32) - rate_a * grad_a).astype(jnp.bfloat16))
        updated_b.append((factor_b.astype(jnp.float32) - rate_b * grad_b).astype(jnp.bfloat16))
    new_a = jnp.stack(updated_a)
    revised_up_factors = jnp.stack(updated_b)
    rank_sum = jnp.einsum('slrd,lkd->slrk', decode_in.astype(jnp.float32), new_a.astype(jnp.float32))
    adapter_rank_size = (rank_sum * scale_a).astype(jnp.bfloat16)
    adapter_weight_change = jnp.einsum('jpax,pxt->jpat', adapter_rank_size.astype(jnp.float32), revised_up_factors.astype(jnp.float32))
    decode_query_matrix = (frozen_query_part.astype(jnp.float32) + up_factor_scale * adapter_weight_change).astype(jnp.bfloat16)
    per_kv = HEADS // KVH
    query_heads = decode_query_matrix.reshape(STEPS, L, ROWS, KVH, per_kv, HD)
    slot_valid = jnp.arange(CTX, dtype=jnp.int32)[None, :] < lengths[:, None]
    causal = jnp.arange(STEPS)[None, :] <= jnp.arange(STEPS)[:, None]
    outputs = []
    for layer_index in range(L):
        cache_keys = kv_cache[layer_index, :, :, :, :HD].astype(jnp.float32)
        cache_values = kv_cache[layer_index, :, :, :, HD:].astype(jnp.float32)
        fresh_keys = new_kv[:, layer_index, :, :, :HD].astype(jnp.float32)
        fresh_values = new_kv[:, layer_index, :, :, HD:].astype(jnp.float32)
        queries = query_heads[:, layer_index].astype(jnp.float32)
        old_scores = jnp.einsum('srkgd,rkpd->srkgp', queries, cache_keys) / math.sqrt(HD)
        old_scores = jnp.where(slot_valid[None, :, None, None, :], old_scores, -jnp.inf)
        new_scores = jnp.einsum('srkgd,trkd->srkgt', queries, fresh_keys) / math.sqrt(HD)
        new_scores = jnp.where(causal[:, None, None, None, :], new_scores, -jnp.inf)
        peak_score = jnp.maximum(lax.optimization_barrier(jnp.max(old_scores, axis=-1)), lax.optimization_barrier(jnp.max(new_scores, axis=-1)))
        old_exp = jnp.exp(old_scores - peak_score[..., None])
        new_exp = jnp.exp(new_scores - peak_score[..., None])
        denominator = lax.optimization_barrier(jnp.sum(old_exp, axis=-1)) + lax.optimization_barrier(jnp.sum(new_exp, axis=-1))
        old_weight = (old_exp / denominator[..., None]).astype(jnp.bfloat16)
        new_weight = (new_exp / denominator[..., None]).astype(jnp.bfloat16)
        layer_out = jnp.einsum('srkgp,rkpd->srkgd', old_weight.astype(jnp.float32), cache_values)
        layer_out = layer_out + jnp.einsum('srkgt,trkd->srkgd', new_weight.astype(jnp.float32), fresh_values)
        outputs.append(layer_out.astype(jnp.bfloat16).reshape(STEPS, ROWS, D))
    attended = jnp.stack(outputs, axis=1)
    return (new_a, revised_up_factors, attended)
```

```python
import math

import jax
import jax.numpy as jnp
from jax import lax
from jax.sharding import PartitionSpec as P

D = 14848
R = 64
GROUPS_PER_COMPLETION = 4

rate_a = 0.5
rate_b = 0.05

f32 = jnp.float32
bf16 = jnp.bfloat16


def pick(array, index, axis=0):
    return lax.dynamic_index_in_dim(array, index, axis, keepdims=False)


def split3(x):
    hi = lax.reduce_precision(x, 8, 7)
    mid = lax.reduce_precision(x - hi, 8, 7)
    lo = lax.reduce_precision(x - hi - mid, 8, 7)
    return hi, mid, lo


def shards(
    activations,
    cotangent,
    rewards,
    group_of,
    layer_owner,
    adapter_a,
    adapter_b,
    frozen_query_part,
    decode_in,
    kv_cache,
    new_kv,
    lengths,
):
    n_dp = lax.axis_size("dp")
    n_tensor = lax.axis_size("tensor")
    chips = n_dp // 2
    index = lax.axis_index("dp")
    core = index % 2
    chip = index // 2
    other = 1 - core
    swap = [(i, i ^ 1) for i in range(n_dp)]
    same_core = [[i for i in range(n_dp) if i % 2 == c] for c in range(2)]
    scale_a = D ** (-0.5)
    scale_b = R ** (-0.5)
    width = activations.shape[2]
    completions = rewards.shape[0]
    tokens = activations.shape[1]

    def core_swap(x):
        return lax.ppermute(x, "dp", swap)

    def across_chips(x):
        return lax.all_to_all(x, "dp", 0, 0, axis_index_groups=same_core)

    def across_tensor(x):
        return lax.all_to_all(x, "tensor", 0, 0)

    own_info = jnp.stack([rewards, group_of.astype(f32)])
    far_info = core_swap(own_info)
    own_factors = jnp.concatenate([pick(adapter_a[0], core), pick(adapter_b[0], core)])
    far_factors = core_swap(
        jnp.concatenate([pick(adapter_a[0], other), pick(adapter_b[0], other)])
    )
    far_act = core_swap(pick(activations, other))
    far_cot = core_swap(pick(cotangent, other))
    far_dec = core_swap(pick(decode_in, other, 1))
    own_act = pick(activations, core)
    own_cot = pick(cotangent, core)
    own_dec = pick(decode_in, core, 1)
    owner = pick(layer_owner, core)
    candidate = jnp.where(owner % 2 == core, own_factors, far_factors)

    info = jnp.concatenate([own_info, far_info], axis=1)
    packed = jnp.concatenate([*split3(info[0]), info[1]]).astype(bf16)
    rows = candidate.shape[0] // chips
    tail = jnp.zeros((rows, 64), bf16).at[0, : packed.shape[0]].set(packed)
    message = jnp.concatenate(
        [candidate.reshape(chips, rows, width), jnp.broadcast_to(tail, (chips, rows, 64))], axis=2
    )
    arrived = across_chips(message)
    piece = pick(arrived, owner // 2)[:, :width]
    infos = arrived[:, 0, width : width + packed.shape[0]].astype(f32)
    infos = infos.reshape(chips, 4, 2 * completions)
    all_rewards = (infos[:, 0] + infos[:, 1] + infos[:, 2]).reshape(-1)
    all_groups = infos[:, 3].reshape(-1)
    labels = jnp.arange(n_dp * completions // GROUPS_PER_COMPLETION, dtype=f32)
    member = (all_groups[:, None] == labels[None, :]).astype(f32)
    group_mean = jnp.sum(member * all_rewards[:, None], axis=0) / jnp.maximum(
        jnp.sum(member, axis=0), 1.0
    )
    mine = (info[1][:, None] == labels[None, :]).astype(f32)
    advantage = info[0] - jnp.sum(mine * group_mean[None, :], axis=1)
    tok_adv = jnp.repeat(advantage, tokens // completions)

    factors = across_chips(jnp.broadcast_to(piece, (chips, rows, width)))
    factors = factors.reshape(chips * rows, width)
    factor_a = factors[:R]
    factor_b = factors[R:]

    def project(factor, x):
        return jnp.einsum("kd,td->kt", factor, x, preferred_element_type=f32)

    low = jnp.concatenate([project(factor_a, own_act), project(factor_a, far_act)], axis=1)
    back = jnp.concatenate([project(factor_b, own_cot), project(factor_b, far_cot)], axis=1)
    parts = jnp.concatenate([low, back]).astype(bf16)
    parts = across_tensor(jnp.broadcast_to(parts, (n_tensor,) + parts.shape))
    sums = jnp.sum(parts.astype(f32), axis=0)
    low_rank = (sums[:R] * scale_a).astype(bf16)
    back_rank = (sums[R:] * (tok_adv * scale_b)[None, :]).astype(bf16)
    low_rank = (low_rank.astype(f32) * tok_adv[None, :]).astype(bf16)

    def grad(rank, own, far):
        return jnp.einsum(
            "kt,td->kd", rank[:, :tokens], own, preferred_element_type=f32
        ) + jnp.einsum("kt,td->kd", rank[:, tokens:], far, preferred_element_type=f32)

    grads = jnp.concatenate(
        [grad(back_rank, own_act, far_act), grad(low_rank, own_cot, far_cot)]
    ).astype(bf16)
    arrived = across_chips(grads.reshape(chips, rows, width))
    step = jnp.where(chip * rows < R, rate_a * scale_a, rate_b * scale_b)
    fresh = (piece.astype(f32) - step * jnp.sum(arrived.astype(f32), axis=0)).astype(bf16)
    fresh = across_chips(jnp.broadcast_to(fresh, (chips, rows, width)))
    fresh = fresh.reshape(chips * rows, width)
    far_fresh = core_swap(fresh)
    first = jnp.where(core == 0, fresh, far_fresh)
    second = jnp.where(core == 0, far_fresh, fresh)
    new_a = jnp.stack([first[:R], second[:R]])
    new_b = jnp.stack([first[R:], second[R:]])

    dec = jnp.stack([own_dec, far_dec])
    rank_part = jnp.einsum(
        "csrd,kd->csrk", dec, fresh[:R], preferred_element_type=f32
    ).astype(bf16)
    rank_part = across_tensor(jnp.broadcast_to(rank_part, (n_tensor,) + rank_part.shape))
    rank_low = (jnp.sum(rank_part.astype(f32), axis=0) * scale_a).astype(bf16)
    far_rank = core_swap(rank_low[1])
    rank_first = jnp.where(core == 0, rank_low[0], far_rank)
    rank_second = jnp.where(core == 0, far_rank, rank_low[0])
    rank_all = jnp.stack([rank_first, rank_second], axis=1)
    change = jnp.einsum("slrk,lkd->slrd", rank_all, new_b, preferred_element_type=f32)
    query = (frozen_query_part.astype(f32) + scale_b * change).astype(bf16)

    steps, layers, rows_dev, _ = query.shape
    kv_local = kv_cache.shape[2]
    slots = kv_cache.shape[3]
    head_dim = kv_cache.shape[4] // 2
    per_kv = width // (kv_local * head_dim)
    query_heads = query.reshape(steps, layers, rows_dev, kv_local, per_kv, head_dim)
    cache_keys = kv_cache[..., :head_dim]
    cache_values = kv_cache[..., head_dim:]
    fresh_keys = new_kv[..., :head_dim]
    fresh_values = new_kv[..., head_dim:]
    old_scores = jnp.einsum(
        "slrkgd,lrkpd->slrkgp", query_heads, cache_keys, preferred_element_type=f32
    ) / math.sqrt(head_dim)
    slot_valid = jnp.arange(slots, dtype=jnp.int32)[None, :] < lengths[:, None]
    old_scores = jnp.where(slot_valid[None, None, :, None, None, :], old_scores, -jnp.inf)
    new_scores = jnp.einsum(
        "slrkgd,tlrkd->slrkgt", query_heads, fresh_keys, preferred_element_type=f32
    ) / math.sqrt(head_dim)
    causal = jnp.arange(steps)[None, :] <= jnp.arange(steps)[:, None]
    new_scores = jnp.where(causal[:, None, None, None, None, :], new_scores, -jnp.inf)
    peak_score = jnp.maximum(jnp.max(old_scores, axis=-1), jnp.max(new_scores, axis=-1))
    old_exp = jnp.exp(old_scores - peak_score[..., None])
    new_exp = jnp.exp(new_scores - peak_score[..., None])
    denominator = jnp.sum(old_exp, axis=-1) + jnp.sum(new_exp, axis=-1)
    old_weight = (old_exp / denominator[..., None]).astype(bf16)
    new_weight = (new_exp / denominator[..., None]).astype(bf16)
    combined = jnp.einsum(
        "slrkgp,lrkpd->slrkgd", old_weight, cache_values, preferred_element_type=f32
    )
    combined = combined + jnp.einsum(
        "slrkgt,tlrkd->slrkgd", new_weight, fresh_values, preferred_element_type=f32
    )
    attended = combined.astype(bf16).reshape(steps, layers, rows_dev, width)
    return (new_a, new_b, attended)


def solution(mesh):
    return jax.shard_map(
        shards,
        mesh=mesh,
        in_specs=(
            P(None, "dp", "tensor"),
            P(None, "dp", "tensor"),
            P("dp"),
            P("dp"),
            P(),
            P("dp", None, None, "tensor"),
            P("dp", None, None, "tensor"),
            P(None, None, "dp", "tensor"),
            P(None, None, "dp", "tensor"),
            P(None, "dp", "tensor", None, None),
            P(None, None, "dp", "tensor", None),
            P("dp"),
        ),
        out_specs=(P(None, None, "tensor"), P(None, None, "tensor"), P(None, None, "dp", "tensor")),
        check_vma=False,
    )
```

```python
import jax
import jax.numpy as jnp
from jax import lax
from jax.experimental import pallas as pl
from jax.experimental.pallas import tpu as pltpu
from jax.sharding import PartitionSpec as P

D = 14848
R = 64
GROUPS_PER_COMPLETION = 4
VMEM_BYTES = 48 * 1024 * 1024

rate_a = 0.5
rate_b = 0.05

f32 = jnp.float32
bf16 = jnp.bfloat16


def pick(array, index, axis=0):
    return lax.dynamic_index_in_dim(array, index, axis, keepdims=False)


def split3(x):
    hi = lax.reduce_precision(x, 8, 7)
    mid = lax.reduce_precision(x - hi, 8, 7)
    lo = lax.reduce_precision(x - hi - mid, 8, 7)
    return hi, mid, lo


def nt_dot(a, b):
    return lax.dot_general(a, b, (((1,), (1,)), ((), ())), preferred_element_type=f32)


def project_kernel(core, factors, act, far_act, cot, far_cot, out):
    r = factors.shape[0] // 2
    tokens = act.shape[2]
    for half, sources in enumerate(((act, far_act), (cot, far_cot))):
        factor = factors[half * r : (half + 1) * r]
        for place, source in enumerate(sources):
            part = jnp.dot(factor, source[0], preferred_element_type=f32).astype(bf16)
            for peer in range(out.shape[0]):
                out[
                    peer, half * r : (half + 1) * r, place * tokens : (place + 1) * tokens
                ] = part


def grad_kernel(core, parts, adv, act, far_act, cot, far_cot, out):
    r = parts.shape[1] // 2
    tokens = act.shape[2]
    total = jnp.sum(parts[...].astype(f32), axis=0)
    low = (total[:r] * D**-0.5).astype(bf16).astype(f32)
    low = (low * adv[...]).astype(bf16)
    back = (total[r:] * (adv[...] * R**-0.5)).astype(bf16)
    for half, (rank, sources) in enumerate(((back, (act, far_act)), (low, (cot, far_cot)))):
        grad = nt_dot(rank[:, :tokens], sources[0][0]) + nt_dot(rank[:, tokens:], sources[1][0])
        out[half * r : (half + 1) * r] = grad.astype(bf16)


def decode_kernel(core, fresh, dec, far_dec, out):
    steps, _, rows, width = dec.shape
    for place, source in enumerate((dec, far_dec)):
        part = nt_dot(fresh[...], source[:, 0].reshape(steps * rows, width)).astype(bf16)
        for peer in range(out.shape[0]):
            out[peer, :, place * steps * rows : (place + 1) * steps * rows] = part


def attend_kernel(rank_ref, up_ref, frozen_ref, kv_ref, new_ref, valid_ref, out_ref, query, result):
    steps, _, rows, width = frozen_ref.shape
    half = query.shape[2] // 2
    heads = width // half
    pad = (query.shape[1] - 8) // steps
    rank = rank_ref[:, 0].reshape(steps * rows, -1)
    change = jnp.dot(rank, up_ref[0], preferred_element_type=f32)
    q = frozen_ref[:, 0].reshape(steps * rows, width).astype(f32) + change * R**-0.5
    q = q.astype(bf16).astype(f32) * (half**-0.5)
    lane = lax.broadcasted_iota(jnp.int32, (steps * rows, 2 * half), 1)
    for pair in range(heads // 2 + heads % 2):
        x = q[:, 2 * half * pair : 2 * half * (pair + 1)]
        if x.shape[1] < 2 * half:
            x = jnp.concatenate([x, jnp.zeros_like(x)], axis=1)
        for odd in range(2):
            head = 2 * pair + odd
            if head >= heads:
                break
            y = jnp.where(lane < half, pltpu.roll(x, half, 1) if odd else x, 0.0)
            for s in range(steps):
                query[:, pad * s + head, :] = y[s * rows : (s + 1) * rows]
    for s in range(steps):
        for head in range(heads, pad):
            query[:, pad * s + head, :] = jnp.zeros((rows, 2 * half), f32)
    place = lax.broadcasted_iota(jnp.int32, (rows, 16, 2 * half), 1)
    tail = jnp.zeros((rows, 16, 2 * half), f32)
    for t in range(steps):
        tail = jnp.where(place == t, new_ref[t, 0].astype(f32)[:, None, :], tail)
    kv = jnp.concatenate([kv_ref[0], tail.astype(bf16)], axis=1)
    scores = jnp.einsum(
        "bqd,bkd->bqk", query[:, : steps * pad].astype(bf16), kv, preferred_element_type=f32
    )
    weights = []
    for s in range(steps):
        mine = scores[:, pad * s : pad * (s + 1)]
        ok = valid_ref[:, s : s + 1, : kv.shape[1]] > 0
        mine = jnp.where(ok, mine, -jnp.inf)
        e = jnp.exp(mine - jnp.max(mine, axis=2, keepdims=True))
        weights.append((e / jnp.sum(e, axis=2, keepdims=True)).astype(bf16))
    weights = jnp.concatenate(weights, axis=1)
    result[:, : steps * pad] = jnp.einsum(
        "bqk,bkd->bqd", weights, kv, preferred_element_type=f32
    )
    low = lax.broadcasted_iota(jnp.int32, (rows, 2 * half), 1) < half
    for s in range(steps):
        for pair in range(heads // 2 + heads % 2):
            head = pad * s + 2 * pair
            even = pltpu.roll(result[:, head, :], half, 1)
            at = 2 * half * pair
            if 2 * pair + 1 < heads:
                both = jnp.where(low, even, result[:, head + 1, :])
                out_ref[s, 0, :, at : at + 2 * half] = both.astype(bf16)
            else:
                out_ref[s, 0, :, at : at + half] = even[:, :half].astype(bf16)


def attend(rank_low, up, frozen, kv, new_kv, valid, rows=32):
    steps, layers, rows_dev, width = frozen.shape
    slots, lanes = kv.shape[2:]
    pad = -(-(width // (lanes // 2)) // 8) * 8
    return pl.pallas_call(
        attend_kernel,
        grid=(layers, rows_dev // rows),
        in_specs=[
            pl.BlockSpec((steps, 1, rows, rank_low.shape[3]), lambda l, r: (0, l, r, 0)),
            pl.BlockSpec((1,) + up.shape[1:], lambda l, r: (l, 0, 0)),
            pl.BlockSpec((steps, 1, rows, width), lambda l, r: (0, l, r, 0)),
            pl.BlockSpec((1, rows, slots, lanes), lambda l, r: (l, r, 0, 0)),
            pl.BlockSpec((steps, 1, rows, lanes), lambda l, r: (0, l, r, 0)),
            pl.BlockSpec((rows, steps, lanes), lambda l, r: (r, 0, 0)),
        ],
        out_specs=pl.BlockSpec((steps, 1, rows, width), lambda l, r: (0, l, r, 0)),
        out_shape=jax.ShapeDtypeStruct(frozen.shape, bf16),
        scratch_shapes=[pltpu.VMEM((rows, steps * pad + 8, lanes), f32)] * 2,
        compiler_params=pltpu.CompilerParams(vmem_limit_bytes=VMEM_BYTES),
        name="attend",
    )(rank_low, up, frozen, kv, new_kv, valid)


def layer_call(kernel, name, core, arrays, layered, out):
    def whole(x):
        return pl.BlockSpec(x.shape, lambda i, c, n=x.ndim: (0,) * n)

    def layer(x, axis):
        shape = tuple(1 if d == axis else n for d, n in enumerate(x.shape))
        return pl.BlockSpec(
            shape, lambda i, c, n=x.ndim: tuple(c[0] if d == axis else 0 for d in range(n))
        )

    return pl.pallas_call(
        kernel,
        grid_spec=pltpu.PrefetchScalarGridSpec(
            num_scalar_prefetch=1,
            grid=(1,),
            in_specs=[whole(x) for x in arrays] + [layer(x, axis) for x, axis in layered],
            out_specs=whole(out),
        ),
        out_shape=out,
        compiler_params=pltpu.CompilerParams(vmem_limit_bytes=VMEM_BYTES),
        name=name,
    )(core.reshape(1), *arrays, *[x for x, _ in layered])


def shards(
    activations,
    cotangent,
    rewards,
    group_of,
    layer_owner,
    adapter_a,
    adapter_b,
    frozen_query_part,
    decode_in,
    kv_cache,
    new_kv,
    lengths,
):
    n_dp = lax.axis_size("dp")
    n_tensor = lax.axis_size("tensor")
    chips = n_dp // 2
    index = lax.axis_index("dp")
    core = index % 2
    chip = index // 2
    swap = [(i, i ^ 1) for i in range(n_dp)]
    same_core = [[i for i in range(n_dp) if i % 2 == c] for c in range(2)]
    layers, tokens, width = activations.shape
    completions = rewards.shape[0]
    steps, _, rows_dev, _ = decode_in.shape
    slots, lanes = kv_cache.shape[3:]

    def core_swap(x):
        return lax.ppermute(x, "dp", swap)

    def across_chips(x):
        return lax.all_to_all(x, "dp", 0, 0, axis_index_groups=same_core)

    def across_tensor(x):
        return lax.all_to_all(x, "tensor", 0, 0)

    own_info = jnp.stack([rewards, group_of.astype(f32)])
    far_a = core_swap(adapter_a)
    far_b = core_swap(adapter_b)
    far_info = core_swap(own_info)
    owner = pick(layer_owner, core)
    is_mine = owner % 2 == core
    candidate = jnp.concatenate(
        [
            jnp.where(is_mine, pick(adapter_a[0], core), pick(far_a[0], core)),
            jnp.where(is_mine, pick(adapter_b[0], core), pick(far_b[0], core)),
        ]
    )

    info = jnp.concatenate([own_info, far_info], axis=1)
    packed = jnp.concatenate([*split3(info[0]), info[1]]).astype(bf16)
    rows = candidate.shape[0] // chips
    tail = jnp.zeros((rows, 64), bf16).at[0, : packed.shape[0]].set(packed)
    message = jnp.concatenate(
        [candidate.reshape(chips, rows, width), jnp.broadcast_to(tail, (chips, rows, 64))], axis=2
    )
    message, act_out, cot_out, dec_out = lax.optimization_barrier(
        (message, activations, cotangent, decode_in)
    )
    arrived = across_chips(message)
    act = jnp.swapaxes(activations, 1, 2)
    cot = jnp.swapaxes(cotangent, 1, 2)
    far_act = core_swap(jnp.swapaxes(act_out, 1, 2))
    far_cot = core_swap(jnp.swapaxes(cot_out, 1, 2))
    far_dec = core_swap(dec_out)
    piece = pick(arrived, owner // 2)[:, :width]
    infos = arrived[:, 0, width : width + packed.shape[0]].astype(f32)
    infos = infos.reshape(chips, 4, 2 * completions)
    all_rewards = (infos[:, 0] + infos[:, 1] + infos[:, 2]).reshape(-1)
    all_groups = infos[:, 3].reshape(-1)
    labels = jnp.arange(n_dp * completions // GROUPS_PER_COMPLETION, dtype=f32)
    member = (all_groups[:, None] == labels[None, :]).astype(f32)
    group_mean = jnp.sum(member * all_rewards[:, None], axis=0) / jnp.maximum(
        jnp.sum(member, axis=0), 1.0
    )
    mine = (info[1][:, None] == labels[None, :]).astype(f32)
    advantage = info[0] - jnp.sum(mine * group_mean[None, :], axis=1)
    tok_adv = jnp.repeat(advantage, tokens // completions)

    factors = across_chips(jnp.broadcast_to(piece, (chips, rows, width)))
    factors = factors.reshape(chips * rows, width)

    token_arrays = [(act, 0), (far_act, 0), (cot, 0), (far_cot, 0)]
    parts = layer_call(
        project_kernel,
        "project",
        core,
        [factors],
        token_arrays,
        jax.ShapeDtypeStruct((n_tensor, 2 * R, 2 * tokens), bf16),
    )
    parts = across_tensor(parts)
    grads = layer_call(
        grad_kernel,
        "grads",
        core,
        [parts, tok_adv.reshape(1, -1)],
        token_arrays,
        jax.ShapeDtypeStruct((2 * R, width), bf16),
    )
    arrived = across_chips(grads.reshape(chips, rows, width))
    step = jnp.where(chip * rows < R, rate_a * D**-0.5, rate_b * R**-0.5)
    fresh = (piece.astype(f32) - step * jnp.sum(arrived.astype(f32), axis=0)).astype(bf16)
    fresh = across_chips(jnp.broadcast_to(fresh, (chips, rows, width)))
    fresh = fresh.reshape(chips * rows, width)

    ranks = layer_call(
        decode_kernel,
        "decode_rank",
        core,
        [fresh[:R]],
        [(decode_in, 1), (far_dec, 1)],
        jax.ShapeDtypeStruct((n_tensor, R, 2 * steps * rows_dev), bf16),
    )
    far_fresh = core_swap(fresh)
    first = jnp.where(core == 0, fresh, far_fresh)
    second = jnp.where(core == 0, far_fresh, fresh)
    new_a = jnp.stack([first[:R], second[:R]])
    new_b = jnp.stack([first[R:], second[R:]])
    ranks = across_tensor(ranks)
    rank_low = (jnp.sum(ranks.astype(f32), axis=0) * D**-0.5).astype(bf16)
    rank_low = rank_low.reshape(R, 2, steps, rows_dev)
    own_rank = rank_low[:, 0]
    far_rank = core_swap(rank_low[:, 1])
    rank_all = jnp.stack(
        [jnp.where(core == 0, own_rank, far_rank), jnp.where(core == 0, far_rank, own_rank)]
    )
    rank_all = jnp.transpose(rank_all, (2, 0, 3, 1))

    column = jnp.arange(lanes)[None, None, :]
    step_of = jnp.arange(steps)[None, :, None]
    valid = column < lengths[:, None, None]
    valid = valid | ((column >= slots) & (column <= slots + step_of))
    attended = attend(
        rank_all,
        new_b,
        frozen_query_part,
        kv_cache.reshape(layers, rows_dev, slots, lanes),
        new_kv.reshape(steps, layers, rows_dev, lanes),
        valid.astype(f32),
    )
    return (new_a, new_b, attended)


def solution(mesh):
    return jax.shard_map(
        shards,
        mesh=mesh,
        in_specs=(
            P(None, "dp", "tensor"),
            P(None, "dp", "tensor"),
            P("dp"),
            P("dp"),
            P(),
            P("dp", None, None, "tensor"),
            P("dp", None, None, "tensor"),
            P(None, None, "dp", "tensor"),
            P(None, None, "dp", "tensor"),
            P(None, "dp", "tensor", None, None),
            P(None, None, "dp", "tensor", None),
            P("dp"),
        ),
        out_specs=(P(None, None, "tensor"), P(None, None, "tensor"), P(None, None, "dp", "tensor")),
        check_vma=False,
    )
```

```python
import jax
import jax.numpy as jnp
from jax import lax
from jax.experimental import pallas as pl
from jax.experimental.pallas import tpu as pltpu
from jax.sharding import PartitionSpec as P

D = 14848
R = 64
GROUPS_PER_COMPLETION = 4
VMEM_BYTES = 32 * 1024 * 1024

rate_a = 0.5
rate_b = 0.05

f32 = jnp.float32
bf16 = jnp.bfloat16


def pick(array, index, axis=0):
    return lax.dynamic_index_in_dim(array, index, axis, keepdims=False)


def split3(x):
    hi = lax.reduce_precision(x, 8, 7)
    mid = lax.reduce_precision(x - hi, 8, 7)
    lo = lax.reduce_precision(x - hi - mid, 8, 7)
    return hi, mid, lo


def nt_dot(a, b):
    return lax.dot_general(a, b, (((1,), (1,)), ((), ())), preferred_element_type=f32)


def in_hbm(x):
    return pltpu.with_memory_space_constraint(x, pltpu.HBM)


def start_all(copies):
    for copy in copies:
        copy.start()
    return copies


def message_kernel(core, owner, own_a, own_b, far_a, far_b, out, both, sems):
    r = own_a.shape[2]

    def run(sources):
        arriving = start_all(
            [
                pltpu.make_async_copy(
                    source.at[0, core[0]], both.at[pl.ds(half * r, r)], sems.at[half]
                )
                for half, source in enumerate(sources)
            ]
        )
        leaving = []
        for half, copy in enumerate(arriving):
            rows = pl.ds(half * r, r)
            copy.wait()
            leaving += start_all(
                [pltpu.make_async_copy(both.at[rows], out.at[rows], sems.at[2 + half])]
            )
        for copy in leaving:
            copy.wait()

    is_mine = owner[core[0]] % 2 == core[0]

    @pl.when(is_mine)
    def _():
        run((own_a, own_b))

    @pl.when(jnp.logical_not(is_mine))
    def _():
        run((far_a, far_b))


def load_tokens(core, sources, held, sems):
    return start_all(
        [
            pltpu.make_async_copy(source.at[core[0]], held.at[i], sems.at[i])
            for i, source in enumerate(sources)
        ]
    )


def project_kernel(core, factors, act, far_act, cot, far_cot, out, held, part, sems, out_sems):
    r = factors.shape[0] // 2
    _, width, tokens = held.shape
    arriving = load_tokens(core, (act, far_act, cot, far_cot), held, sems)
    leaving = []
    for half in range(2):
        rows = pl.ds(half * r, r)
        factor = factors[half * r : (half + 1) * r, :width]
        for place in range(2):
            arriving[2 * half + place].wait()
            part[rows, place * tokens : (place + 1) * tokens] = jnp.dot(
                factor, held[2 * half + place], preferred_element_type=f32
            ).astype(bf16)
        leaving += start_all(
            [
                pltpu.make_async_copy(part.at[rows], out.at[peer, rows], out_sems.at[half, peer])
                for peer in range(out.shape[0])
            ]
        )
    for copy in leaving:
        copy.wait()


def grad_kernel(core, advantage, parts, act, far_act, cot, far_cot, out, held, sems):
    r = parts.shape[1] // 2
    _, width, tokens = held.shape
    arriving = load_tokens(core, (act, far_act, cot, far_cot), held, sems)
    count = advantage.shape[0]
    sequence = lax.broadcasted_iota(jnp.int32, (1, 2 * tokens), 1) // (2 * tokens // count)
    adv = jnp.zeros(sequence.shape, f32)
    for i in range(count):
        adv = jnp.where(sequence == i, advantage[i], adv)
    total = jnp.sum(parts[...].astype(f32), axis=0)
    low = (total[:r] * D**-0.5).astype(bf16).astype(f32)
    low = (low * adv).astype(bf16)
    back = (total[r:] * (adv * R**-0.5)).astype(bf16)
    for half, rank in enumerate((back, low)):
        arriving[2 * half].wait()
        grad = nt_dot(rank[:, :tokens], held[2 * half])
        arriving[2 * half + 1].wait()
        grad += nt_dot(rank[:, tokens:], held[2 * half + 1])
        out[half * r : (half + 1) * r] = grad.astype(bf16)


def decode_kernel(core, fresh, dec, far_dec, out):
    steps, _, rows, width = dec.shape
    mine, other = core[0], 1 - core[0]
    for place, source in ((mine, dec), (other, far_dec)):
        part = nt_dot(fresh[: out.shape[2]], source[:, 0].reshape(steps * rows, width)).astype(bf16)
        for peer in range(out.shape[0]):
            out[peer, place] = part


def attend_kernel(
    core,
    rank_ref,
    fresh,
    far_fresh,
    frozen_ref,
    kv_ref,
    new_ref,
    valid_ref,
    new_a,
    new_b,
    out_ref,
    change,
):
    steps, _, rows, width = frozen_ref.shape
    half = kv_ref.shape[3] // 2
    heads = width // half
    pad = -(-heads // 8) * 8
    layer, block = pl.program_id(0), pl.program_id(1)

    def begin(source):
        new_a[0] = source[:R]
        new_b[0] = source[R:]
        rank = (jnp.sum(rank_ref[:, 0].astype(f32), axis=0) * D**-0.5).astype(bf16)
        change[...] = lax.dot_general(
            rank, source[R:], (((0,), (0,)), ((), ())), preferred_element_type=f32
        ).reshape(change.shape)

    @pl.when((block == 0) & (layer == core[0]))
    def _():
        begin(fresh)

    @pl.when((block == 0) & (layer != core[0]))
    def _():
        begin(far_fresh)

    delta = change[:, pl.ds(block * rows, rows)].reshape(steps * rows, width)
    q = frozen_ref[:, 0].reshape(steps * rows, width).astype(f32) + delta * R**-0.5
    q = q.astype(bf16).astype(f32) * (half**-0.5)
    lane = lax.broadcasted_iota(jnp.int32, (steps * rows, 2 * half), 1)
    pieces = [[jnp.zeros((rows, 2 * half), f32)] * pad for _ in range(steps)]
    for pair in range(heads // 2 + heads % 2):
        x = q[:, 2 * half * pair : 2 * half * (pair + 1)]
        if x.shape[1] < 2 * half:
            x = jnp.concatenate([x, jnp.zeros_like(x)], axis=1)
        for odd in range(2):
            head = 2 * pair + odd
            if head >= heads:
                break
            y = jnp.where(lane < half, pltpu.roll(x, half, 1) if odd else x, 0.0)
            for s in range(steps):
                pieces[s][head] = y[s * rows : (s + 1) * rows]
    query = jnp.transpose(jnp.stack(sum(pieces, [])), (1, 0, 2)).astype(bf16)
    place = lax.broadcasted_iota(jnp.int32, (rows, 16, 2 * half), 1)
    tail = jnp.zeros((rows, 16, 2 * half), f32)
    for t in range(steps):
        tail = jnp.where(place == t, new_ref[t, 0].astype(f32)[:, None, :], tail)
    kv = jnp.concatenate([kv_ref[0], tail.astype(bf16)], axis=1)
    scores = jnp.einsum("bqd,bkd->bqk", query, kv, preferred_element_type=f32)
    weights = []
    for s in range(steps):
        mine = scores[:, pad * s : pad * (s + 1)]
        ok = valid_ref[:, s : s + 1, : kv.shape[1]] > 0
        mine = jnp.where(ok, mine, -jnp.inf)
        e = jnp.exp(mine - jnp.max(mine, axis=2, keepdims=True))
        weights.append((e / jnp.sum(e, axis=2, keepdims=True)).astype(bf16))
    weights = jnp.concatenate(weights, axis=1)
    result = jnp.einsum("bqk,bkd->bqd", weights, kv, preferred_element_type=f32)
    result = jnp.transpose(result, (1, 0, 2))
    low = lax.broadcasted_iota(jnp.int32, (rows, 2 * half), 1) < half
    for s in range(steps):
        for pair in range(heads // 2 + heads % 2):
            head = pad * s + 2 * pair
            even = pltpu.roll(result[head], half, 1)
            at = 2 * half * pair
            if 2 * pair + 1 < heads:
                both = jnp.where(low, even, result[head + 1])
                out_ref[s, 0, :, at : at + 2 * half] = both.astype(bf16)
            else:
                out_ref[s, 0, :, at : at + half] = even[:, :half].astype(bf16)


def attend(core, ranks, fresh, far_fresh, frozen, kv, new_kv, valid, rows=32):
    steps, layers, rows_dev, width = frozen.shape
    slots, lanes = kv.shape[2:]
    factor = jax.ShapeDtypeStruct((layers, R, width), bf16)
    return pl.pallas_call(
        attend_kernel,
        grid_spec=pltpu.PrefetchScalarGridSpec(
            num_scalar_prefetch=1,
            grid=(layers, rows_dev // rows),
            in_specs=[
                pl.BlockSpec((ranks.shape[0], 1) + ranks.shape[2:], lambda l, r, c: (0, l, 0, 0)),
                pl.BlockSpec(fresh.shape, lambda l, r, c: (0, 0)),
                pl.BlockSpec(fresh.shape, lambda l, r, c: (0, 0)),
                pl.BlockSpec((steps, 1, rows, width), lambda l, r, c: (0, l, r, 0)),
                pl.BlockSpec((1, rows, slots, lanes), lambda l, r, c: (l, r, 0, 0)),
                pl.BlockSpec((steps, 1, rows, lanes), lambda l, r, c: (0, l, r, 0)),
                pl.BlockSpec((rows, steps, lanes), lambda l, r, c: (r, 0, 0)),
            ],
            out_specs=[
                pl.BlockSpec((1, R, width), lambda l, r, c: (l, 0, 0)),
                pl.BlockSpec((1, R, width), lambda l, r, c: (l, 0, 0)),
                pl.BlockSpec((steps, 1, rows, width), lambda l, r, c: (0, l, r, 0)),
            ],
            scratch_shapes=[pltpu.VMEM((steps, rows_dev, width), f32)],
        ),
        out_shape=[factor, factor, jax.ShapeDtypeStruct(frozen.shape, bf16)],
        compiler_params=pltpu.CompilerParams(vmem_limit_bytes=VMEM_BYTES),
        name="attend",
    )(core.reshape(1), ranks, fresh, far_fresh, frozen, kv, new_kv, valid)


def layer_call(kernel, name, core, arrays, layered, out):
    def whole(x):
        return pl.BlockSpec(x.shape, lambda i, c, n=len(x.shape): (0,) * n)

    def layer(x, axis):
        shape = tuple(1 if d == axis else n for d, n in enumerate(x.shape))
        return pl.BlockSpec(
            shape, lambda i, c, n=x.ndim: tuple(c[0] if d == axis else 0 for d in range(n))
        )

    return pl.pallas_call(
        kernel,
        grid_spec=pltpu.PrefetchScalarGridSpec(
            num_scalar_prefetch=1,
            grid=(1,),
            in_specs=[whole(x) for x in arrays] + [layer(x, axis) for x, axis in layered],
            out_specs=whole(out),
        ),
        out_shape=pltpu.HBM(out.shape, out.dtype),
        compiler_params=pltpu.CompilerParams(vmem_limit_bytes=VMEM_BYTES),
        name=name,
    )(core.reshape(1), *arrays, *[x for x, _ in layered])


def local_call(kernel, name, scalars, whole, streamed, out, scratch, by_copy=True):
    def block(shape):
        return pl.BlockSpec(shape, lambda i, *_: (0,) * len(shape))

    return pl.pallas_call(
        kernel,
        grid_spec=pltpu.PrefetchScalarGridSpec(
            num_scalar_prefetch=len(scalars),
            grid=(1,),
            in_specs=[block(x.shape) for x in whole]
            + [pl.BlockSpec(memory_space=pl.ANY)] * len(streamed),
            out_specs=pl.BlockSpec(memory_space=pl.ANY) if by_copy else block(out),
            scratch_shapes=scratch,
        ),
        out_shape=pltpu.HBM(out, bf16),
        compiler_params=pltpu.CompilerParams(vmem_limit_bytes=VMEM_BYTES),
        name=name,
    )(*scalars, *whole, *streamed)


def shards(
    activations,
    cotangent,
    rewards,
    group_of,
    layer_owner,
    adapter_a,
    adapter_b,
    frozen_query_part,
    decode_in,
    kv_cache,
    new_kv,
    lengths,
):
    n_dp = lax.axis_size("dp")
    n_tensor = lax.axis_size("tensor")
    chips = n_dp // 2
    index = lax.axis_index("dp")
    core = index % 2
    chip = index // 2
    swap = [(i, i ^ 1) for i in range(n_dp)]
    same_core = [[i for i in range(n_dp) if i % 2 == c] for c in range(2)]
    layers, tokens, width = activations.shape
    completions = rewards.shape[0]
    steps, _, rows_dev, _ = decode_in.shape
    slots, lanes = kv_cache.shape[3:]

    def core_swap(x):
        return lax.ppermute(x, "dp", swap)

    def across_chips(x):
        return lax.all_to_all(x, "dp", 0, 0, axis_index_groups=same_core)

    def across_tensor(x):
        return lax.all_to_all(x, "tensor", 0, 0)

    far_a = core_swap(adapter_a)
    far_b = core_swap(adapter_b)
    scalars = [core.reshape(1)]
    candidate = local_call(
        message_kernel,
        "message",
        scalars + [in_hbm(layer_owner)],
        [],
        [in_hbm(adapter_a), in_hbm(adapter_b), far_a, far_b],
        (2 * R, width),
        [pltpu.VMEM((2 * R, width), bf16), pltpu.SemaphoreType.DMA((4,))],
    )
    rows = candidate.shape[0] // chips

    message, act_out, cot_out, dec_out, rewards, group_of = lax.optimization_barrier(
        (
            candidate.reshape(chips, rows, width),
            activations,
            cotangent,
            decode_in,
            rewards,
            group_of,
        )
    )
    arrived = across_chips(message)
    act = jnp.swapaxes(activations, 1, 2)
    cot = jnp.swapaxes(cotangent, 1, 2)
    own_info = jnp.stack([rewards, group_of.astype(f32)])
    far_info = core_swap(own_info)
    far_act = core_swap(jnp.swapaxes(act_out, 1, 2))
    far_cot = core_swap(jnp.swapaxes(cot_out, 1, 2))
    far_dec = core_swap(dec_out)
    piece = pick(arrived, pick(layer_owner, core) // 2)

    info = jnp.concatenate([own_info, far_info], axis=1)
    packed = jnp.concatenate([*split3(info[0]), info[1]]).astype(bf16)
    tail = jnp.zeros((rows, 64), bf16).at[0, : packed.shape[0]].set(packed)
    message = jnp.concatenate([piece, tail], axis=1)
    factors = across_chips(jnp.broadcast_to(message, (chips,) + message.shape))
    infos = factors[:, 0, width : width + packed.shape[0]].astype(f32)
    infos = infos.reshape(chips, 4, 2 * completions)
    all_rewards = (infos[:, 0] + infos[:, 1] + infos[:, 2]).reshape(-1)
    all_groups = infos[:, 3].reshape(-1)
    labels = jnp.arange(n_dp * completions // GROUPS_PER_COMPLETION, dtype=f32)
    member = (all_groups[:, None] == labels[None, :]).astype(f32)
    group_mean = jnp.sum(member * all_rewards[:, None], axis=0) / jnp.maximum(
        jnp.sum(member, axis=0), 1.0
    )
    mine = (info[1][:, None] == labels[None, :]).astype(f32)
    advantage = info[0] - jnp.sum(mine * group_mean[None, :], axis=1)
    factors = factors.reshape(chips * rows, -1)

    token_arrays = [in_hbm(act), far_act, in_hbm(cot), far_cot]
    token_scratch = [pltpu.VMEM((4, width, tokens), bf16), pltpu.SemaphoreType.DMA((4,))]
    parts = local_call(
        project_kernel,
        "project",
        scalars,
        [factors],
        token_arrays,
        (n_tensor, 2 * R, 2 * tokens),
        token_scratch[:1]
        + [pltpu.VMEM((2 * R, 2 * tokens), bf16)]
        + token_scratch[1:]
        + [pltpu.SemaphoreType.DMA((2, n_tensor))],
    )
    parts = across_tensor(parts)
    grads = local_call(
        grad_kernel,
        "grads",
        scalars + [advantage],
        [parts],
        token_arrays,
        (2 * R, width),
        token_scratch,
        by_copy=False,
    )
    arrived = across_chips(grads.reshape(chips, rows, width))
    step = jnp.where(chip * rows < R, rate_a * D**-0.5, rate_b * R**-0.5)
    fresh = (piece.astype(f32) - step * jnp.sum(arrived.astype(f32), axis=0)).astype(bf16)
    fresh = across_chips(jnp.broadcast_to(fresh, (chips, rows, width)))
    fresh = fresh.reshape(chips * rows, width)

    ranks = layer_call(
        decode_kernel,
        "decode_rank",
        core,
        [fresh],
        [(decode_in, 1), (far_dec, 1)],
        jax.ShapeDtypeStruct((n_tensor, 2, R, steps * rows_dev), bf16),
    )
    far_fresh = core_swap(fresh)
    ranks = lax.all_to_all(
        ranks.reshape(n_tensor * 2, R, steps * rows_dev),
        ("dp", "tensor"),
        0,
        0,
        axis_index_groups=[
            [(pair * 2 + c) * n_tensor + t for t in range(n_tensor) for c in range(2)]
            for pair in range(chips)
        ],
    ).reshape(n_tensor, 2, R, steps * rows_dev)

    column = jnp.arange(lanes)[None, None, :]
    step_of = jnp.arange(steps)[None, :, None]
    valid = column < lengths[:, None, None]
    valid = valid | ((column >= slots) & (column <= slots + step_of))
    return attend(
        core,
        ranks,
        fresh,
        far_fresh,
        in_hbm(frozen_query_part),
        in_hbm(kv_cache.reshape(layers, rows_dev, slots, lanes)),
        new_kv.reshape(steps, layers, rows_dev, lanes),
        valid.astype(f32),
    )


def solution(mesh):
    return jax.shard_map(
        shards,
        mesh=mesh,
        in_specs=(
            P(None, "dp", "tensor"),
            P(None, "dp", "tensor"),
            P("dp"),
            P("dp"),
            P(),
            P("dp", None, None, "tensor"),
            P("dp", None, None, "tensor"),
            P(None, None, "dp", "tensor"),
            P(None, None, "dp", "tensor"),
            P(None, "dp", "tensor", None, None),
            P(None, None, "dp", "tensor", None),
            P("dp"),
        ),
        out_specs=(P(None, None, "tensor"), P(None, None, "tensor"), P(None, None, "dp", "tensor")),
        check_vma=False,
    )
```

```python
import jax
import jax.numpy as jnp
from jax import lax
from jax.experimental import pallas as pl
from jax.experimental.pallas import tpu as pltpu
from jax.sharding import PartitionSpec as P

D = 14848
R = 64
ROWS = 8
TAIL = D // 8 % 128
VMEM_BYTES = 32 * 1024 * 1024

rate_a = 0.5
rate_b = 0.05

f32 = jnp.float32
bf16 = jnp.bfloat16


def pick(array, index, axis=0):
    return lax.dynamic_index_in_dim(array, index, axis, keepdims=False)


def split3(x):
    hi = lax.reduce_precision(x, 8, 7)
    mid = lax.reduce_precision(x - hi, 8, 7)
    lo = lax.reduce_precision(x - hi - mid, 8, 7)
    return hi, mid, lo


def nt_dot(a, b):
    return lax.dot_general(a, b, (((1,), (1,)), ((), ())), preferred_element_type=f32)


def in_hbm(x):
    return pltpu.with_memory_space_constraint(x, pltpu.HBM)


def start_all(copies):
    for copy in copies:
        copy.start()
    return copies


def message_kernel(core, owner, own_a, own_b, far_a, far_b, out, both, sems):
    r = own_a.shape[2]

    def run(sources):
        arriving = start_all(
            [
                pltpu.make_async_copy(
                    source.at[0, core[0]], both.at[pl.ds(half * r, r)], sems.at[half]
                )
                for half, source in enumerate(sources)
            ]
        )
        leaving = []
        for half, copy in enumerate(arriving):
            rows = pl.ds(half * r, r)
            copy.wait()
            leaving += start_all(
                [pltpu.make_async_copy(both.at[rows], out.at[rows], sems.at[2 + half])]
            )
        for copy in leaving:
            copy.wait()

    is_mine = owner[core[0]] % 2 == core[0]

    @pl.when(is_mine)
    def _():
        run((own_a, own_b))

    @pl.when(jnp.logical_not(is_mine))
    def _():
        run((far_a, far_b))


def load_tokens(core, sources, held, sems):
    return start_all(
        [
            pltpu.make_async_copy(source.at[core[0]], held.at[i], sems.at[i])
            for i, source in enumerate(sources)
        ]
    )


def token_advantage(info, tails, count, tokens):
    lanes = tails.shape[1]

    def lane_shifted(x, by):
        return pltpu.roll(x, lanes - by, 1)

    rewards = tails + lane_shifted(tails, count) + lane_shifted(tails, 2 * count)
    groups = lane_shifted(tails, 3 * count)
    row = lax.broadcasted_iota(jnp.int32, tails.shape, 0)
    lane = lax.broadcasted_iota(jnp.int32, tails.shape, 1)
    used = (row % ROWS == 0) & (lane >= TAIL) & (lane < TAIL + count)
    sequence = lax.broadcasted_iota(jnp.int32, (1, tokens), 1) // (tokens // count)
    adv = jnp.zeros(sequence.shape, f32)
    for i in range(count):
        same = used & (groups == info[count + i])
        total = jnp.sum(jnp.where(same, rewards, 0.0), keepdims=True)
        members = jnp.sum(jnp.where(same, 1.0, 0.0), keepdims=True)
        adv = jnp.where(sequence == i, info[i] - total / jnp.maximum(members, 1.0), adv)
    return adv


def project_kernel(
    core, info, factors, act, far_act, cot, far_cot, out, adv, held, part, sems, out_sems
):
    r = factors.shape[0] // 2
    _, width, tokens = held.shape
    arriving = load_tokens(core, (act, far_act, cot, far_cot), held, sems)
    tails = factors[:, width // 128 * 128 :].astype(f32)
    adv[...] = token_advantage(info, tails, info.shape[0] // 2, 2 * tokens)
    leaving = []
    for half in range(2):
        rows = pl.ds(half * r, r)
        factor = factors[half * r : (half + 1) * r, :width]
        for place in range(2):
            arriving[2 * half + place].wait()
            part[rows, place * tokens : (place + 1) * tokens] = jnp.dot(
                factor, held[2 * half + place], preferred_element_type=f32
            ).astype(bf16)
        leaving += start_all(
            [
                pltpu.make_async_copy(part.at[rows], out.at[peer, rows], out_sems.at[half, peer])
                for peer in range(out.shape[0])
            ]
        )
    for copy in leaving:
        copy.wait()


def grad_kernel(core, parts, adv_ref, act, far_act, cot, far_cot, out, held, sems):
    r = parts.shape[1] // 2
    _, width, tokens = held.shape
    arriving = load_tokens(core, (act, far_act, cot, far_cot), held, sems)
    adv = adv_ref[...]
    total = jnp.sum(parts[...].astype(f32), axis=0)
    low = (total[:r] * D**-0.5).astype(bf16).astype(f32)
    low = (low * adv).astype(bf16)
    back = (total[r:] * (adv * R**-0.5)).astype(bf16)
    for half, rank in enumerate((back, low)):
        arriving[2 * half].wait()
        grad = nt_dot(rank[:, :tokens], held[2 * half])
        arriving[2 * half + 1].wait()
        grad += nt_dot(rank[:, tokens:], held[2 * half + 1])
        out[half * r : (half + 1) * r] = grad.astype(bf16)


def update_kernel(chip, arrived, piece, out):
    total = jnp.sum(arrived[...].astype(f32), axis=0)
    step = jnp.where(chip[0] * ROWS < R, rate_a * D**-0.5, rate_b * R**-0.5)
    fresh = (piece[...].astype(f32) - step * total).astype(bf16)
    for peer in range(out.shape[0]):
        out[peer] = fresh


def decode_kernel(core, fresh, dec, far_dec, out):
    steps, rows, width = dec.shape
    mine, other = core[0], 1 - core[0]
    for place, source in ((mine, dec), (other, far_dec)):
        part = nt_dot(fresh[: out.shape[2]], source[...].reshape(steps * rows, width)).astype(bf16)
        for peer in range(out.shape[0]):
            out[peer, place] = part


def attend_kernel(
    core,
    rank_ref,
    fresh,
    far_fresh,
    frozen_ref,
    kv_ref,
    new_ref,
    valid_ref,
    new_a,
    new_b,
    out_ref,
    change,
):
    steps, _, rows, width = frozen_ref.shape
    half = kv_ref.shape[3] // 2
    heads = width // half
    pad = -(-heads // 8) * 8
    layer, block = pl.program_id(0), pl.program_id(1)

    def begin(source):
        new_a[0] = source[:R]
        new_b[0] = source[R:]
        rank = (jnp.sum(rank_ref[:, 0].astype(f32), axis=0) * D**-0.5).astype(bf16)
        change[...] = lax.dot_general(
            rank, source[R:], (((0,), (0,)), ((), ())), preferred_element_type=f32
        ).reshape(change.shape)

    @pl.when((block == 0) & (layer == core[0]))
    def _():
        begin(fresh)

    @pl.when((block == 0) & (layer != core[0]))
    def _():
        begin(far_fresh)

    delta = change[:, pl.ds(block * rows, rows)].reshape(steps * rows, width)
    q = frozen_ref[:, 0].reshape(steps * rows, width).astype(f32) + delta * R**-0.5
    q = q.astype(bf16).astype(f32) * (half**-0.5)
    lane = lax.broadcasted_iota(jnp.int32, (steps * rows, 2 * half), 1)
    pieces = [[jnp.zeros((rows, 2 * half), f32)] * pad for _ in range(steps)]
    for pair in range(heads // 2 + heads % 2):
        x = q[:, 2 * half * pair : 2 * half * (pair + 1)]
        if x.shape[1] < 2 * half:
            x = jnp.concatenate([x, jnp.zeros_like(x)], axis=1)
        for odd in range(2):
            head = 2 * pair + odd
            if head >= heads:
                break
            y = jnp.where(lane < half, pltpu.roll(x, half, 1) if odd else x, 0.0)
            for s in range(steps):
                pieces[s][head] = y[s * rows : (s + 1) * rows]
    query = jnp.transpose(jnp.stack(sum(pieces, [])), (1, 0, 2)).astype(bf16)
    place = lax.broadcasted_iota(jnp.int32, (rows, 16, 2 * half), 1)
    tail = jnp.zeros((rows, 16, 2 * half), f32)
    for t in range(steps):
        tail = jnp.where(place == t, new_ref[t, 0].astype(f32)[:, None, :], tail)
    kv = jnp.concatenate([kv_ref[0], tail.astype(bf16)], axis=1)
    scores = jnp.einsum("bqd,bkd->bqk", query, kv, preferred_element_type=f32)
    weights = []
    for s in range(steps):
        mine = scores[:, pad * s : pad * (s + 1)]
        ok = valid_ref[:, s : s + 1, : kv.shape[1]] > 0
        mine = jnp.where(ok, mine, -jnp.inf)
        e = jnp.exp(mine - jnp.max(mine, axis=2, keepdims=True))
        weights.append((e / jnp.sum(e, axis=2, keepdims=True)).astype(bf16))
    weights = jnp.concatenate(weights, axis=1)
    result = jnp.einsum("bqk,bkd->bqd", weights, kv, preferred_element_type=f32)
    result = jnp.transpose(result, (1, 0, 2))
    low = lax.broadcasted_iota(jnp.int32, (rows, 2 * half), 1) < half
    for s in range(steps):
        for pair in range(heads // 2 + heads % 2):
            head = pad * s + 2 * pair
            even = pltpu.roll(result[head], half, 1)
            at = 2 * half * pair
            if 2 * pair + 1 < heads:
                both = jnp.where(low, even, result[head + 1])
                out_ref[s, 0, :, at : at + 2 * half] = both.astype(bf16)
            else:
                out_ref[s, 0, :, at : at + half] = even[:, :half].astype(bf16)


def attend(core, ranks, fresh, far_fresh, frozen, kv, new_kv, valid, rows=32):
    steps, layers, rows_dev, width = frozen.shape
    slots, lanes = kv.shape[2:]
    factor = jax.ShapeDtypeStruct((layers, R, width), bf16)
    return pl.pallas_call(
        attend_kernel,
        grid_spec=pltpu.PrefetchScalarGridSpec(
            num_scalar_prefetch=1,
            grid=(layers, rows_dev // rows),
            in_specs=[
                pl.BlockSpec((ranks.shape[0], 1) + ranks.shape[2:], lambda l, r, c: (0, l, 0, 0)),
                pl.BlockSpec(fresh.shape, lambda l, r, c: (0, 0)),
                pl.BlockSpec(fresh.shape, lambda l, r, c: (0, 0)),
                pl.BlockSpec((steps, 1, rows, width), lambda l, r, c: (0, l, r, 0)),
                pl.BlockSpec((1, rows, slots, lanes), lambda l, r, c: (l, r, 0, 0)),
                pl.BlockSpec((steps, 1, rows, lanes), lambda l, r, c: (0, l, r, 0)),
                pl.BlockSpec((rows, steps, lanes), lambda l, r, c: (r, 0, 0)),
            ],
            out_specs=[
                pl.BlockSpec((1, R, width), lambda l, r, c: (l, 0, 0)),
                pl.BlockSpec((1, R, width), lambda l, r, c: (l, 0, 0)),
                pl.BlockSpec((steps, 1, rows, width), lambda l, r, c: (0, l, r, 0)),
            ],
            scratch_shapes=[pltpu.VMEM((steps, rows_dev, width), f32)],
        ),
        out_shape=[factor, factor, jax.ShapeDtypeStruct(frozen.shape, bf16)],
        compiler_params=pltpu.CompilerParams(vmem_limit_bytes=VMEM_BYTES),
        name="attend",
    )(core.reshape(1), ranks, fresh, far_fresh, frozen, kv, new_kv, valid)


def local_call(kernel, name, scalars, whole, streamed, out, scratch, by_copy=True, beside=None):
    def block(shape):
        return pl.BlockSpec(shape, lambda i, *_: (0,) * len(shape))

    out_spec = pl.BlockSpec(memory_space=pl.ANY) if by_copy else block(out)
    return pl.pallas_call(
        kernel,
        grid_spec=pltpu.PrefetchScalarGridSpec(
            num_scalar_prefetch=len(scalars),
            grid=(1,),
            in_specs=[block(x.shape) for x in whole]
            + [pl.BlockSpec(memory_space=pl.ANY)] * len(streamed),
            out_specs=(out_spec, block(beside.shape)) if beside else out_spec,
            scratch_shapes=scratch,
        ),
        out_shape=(pltpu.HBM(out, bf16), beside) if beside else pltpu.HBM(out, bf16),
        compiler_params=pltpu.CompilerParams(vmem_limit_bytes=VMEM_BYTES),
        name=name,
    )(*scalars, *whole, *streamed)


def shards(
    activations,
    cotangent,
    rewards,
    group_of,
    layer_owner,
    adapter_a,
    adapter_b,
    frozen_query_part,
    decode_in,
    kv_cache,
    new_kv,
    lengths,
):
    n_dp = lax.axis_size("dp")
    n_tensor = lax.axis_size("tensor")
    chips = n_dp // 2
    index = lax.axis_index("dp")
    core = index % 2
    chip = index // 2
    swap = [(i, i ^ 1) for i in range(n_dp)]
    same_core = [[i for i in range(n_dp) if i % 2 == c] for c in range(2)]
    layers, tokens, width = activations.shape
    completions = rewards.shape[0]
    steps, _, rows_dev, _ = decode_in.shape
    slots, lanes = kv_cache.shape[3:]

    def core_swap(x):
        return lax.ppermute(x, "dp", swap)

    def across_chips(x):
        return lax.all_to_all(x, "dp", 0, 0, axis_index_groups=same_core)

    def across_tensor(x):
        return lax.all_to_all(x, "tensor", 0, 0)

    far_a = core_swap(adapter_a)
    far_b = core_swap(adapter_b)
    scalars = [core.reshape(1)]
    candidate = local_call(
        message_kernel,
        "message",
        scalars + [in_hbm(layer_owner)],
        [],
        [in_hbm(adapter_a), in_hbm(adapter_b), far_a, far_b],
        (2 * R, width),
        [pltpu.VMEM((2 * R, width), bf16), pltpu.SemaphoreType.DMA((4,))],
    )
    rows = ROWS

    message, layer_owner, act_out, cot_out, dec_out, rewards, group_of = lax.optimization_barrier(
        (
            candidate.reshape(chips, rows, width),
            layer_owner,
            activations,
            cotangent,
            decode_in,
            rewards,
            group_of,
        )
    )
    arrived = across_chips(message)
    act = jnp.swapaxes(activations, 1, 2)
    cot = jnp.swapaxes(cotangent, 1, 2)
    own_info = jnp.stack([rewards, group_of.astype(f32)])
    far_info = core_swap(own_info)
    far_act = core_swap(jnp.swapaxes(act_out, 1, 2))
    far_cot = core_swap(jnp.swapaxes(cot_out, 1, 2))
    dec = pick(dec_out, core, 1)
    far_dec = core_swap(pick(dec_out, 1 - core, 1))
    column = jnp.arange(lanes)[None, None, :]
    step_of = jnp.arange(steps)[None, :, None]
    valid = column < lengths[:, None, None]
    valid = valid | ((column >= slots) & (column <= slots + step_of))
    info = jnp.concatenate([own_info, far_info], axis=1)
    packed = jnp.concatenate([*split3(info[0]), info[1]]).astype(bf16)
    tail = jnp.zeros((rows, 64), bf16).at[0, : packed.shape[0]].set(packed)
    owner_chip = pick(layer_owner, core) // 2
    arrived, owner_chip, tail, info, valid, dec, far_dec, far_act, far_cot = (
        lax.optimization_barrier(
            (arrived, owner_chip, tail, info, valid.astype(f32), dec, far_dec, far_act, far_cot)
        )
    )
    piece = pick(arrived, owner_chip)

    message = jnp.concatenate([piece, tail], axis=1)
    factors = across_chips(jnp.broadcast_to(message, (chips,) + message.shape))
    factors = factors.reshape(chips * rows, -1)

    token_arrays = [act, far_act, in_hbm(cot), far_cot]
    token_scratch = [pltpu.VMEM((4, width, tokens), bf16), pltpu.SemaphoreType.DMA((4,))]
    parts, advantage = local_call(
        project_kernel,
        "project",
        scalars + [info.reshape(-1)],
        [factors],
        token_arrays,
        (n_tensor, 2 * R, 2 * tokens),
        token_scratch[:1]
        + [pltpu.VMEM((2 * R, 2 * tokens), bf16)]
        + token_scratch[1:]
        + [pltpu.SemaphoreType.DMA((2, n_tensor))],
        beside=jax.ShapeDtypeStruct((1, 2 * tokens), f32),
    )
    parts = across_tensor(parts)
    grads = local_call(
        grad_kernel,
        "grads",
        scalars,
        [parts, advantage],
        token_arrays,
        (2 * R, width),
        token_scratch,
        by_copy=False,
    )
    arrived = across_chips(grads.reshape(chips, rows, width))
    fresh = local_call(
        update_kernel,
        "update",
        [chip.reshape(1)],
        [arrived, piece],
        [],
        (chips, rows, width),
        [],
        by_copy=False,
    )
    fresh = across_chips(fresh)
    fresh = fresh.reshape(chips * rows, width)

    ranks = local_call(
        decode_kernel,
        "decode_rank",
        scalars,
        [fresh, dec, far_dec],
        [],
        (n_tensor, 2, R, steps * rows_dev),
        [],
        by_copy=False,
    )
    far_fresh = core_swap(fresh)
    ranks = lax.all_to_all(
        ranks.reshape(n_tensor * 2, R, steps * rows_dev),
        ("dp", "tensor"),
        0,
        0,
        axis_index_groups=[
            [(pair * 2 + c) * n_tensor + t for t in range(n_tensor) for c in range(2)]
            for pair in range(chips)
        ],
    ).reshape(n_tensor, 2, R, steps * rows_dev)

    return attend(
        core,
        ranks,
        fresh,
        far_fresh,
        in_hbm(frozen_query_part),
        in_hbm(kv_cache.reshape(layers, rows_dev, slots, lanes)),
        new_kv.reshape(steps, layers, rows_dev, lanes),
        valid,
    )


def solution(mesh):
    return jax.shard_map(
        shards,
        mesh=mesh,
        in_specs=(
            P(None, "dp", "tensor"),
            P(None, "dp", "tensor"),
            P("dp"),
            P("dp"),
            P(),
            P("dp", None, None, "tensor"),
            P("dp", None, None, "tensor"),
            P(None, None, "dp", "tensor"),
            P(None, None, "dp", "tensor"),
            P(None, "dp", "tensor", None, None),
            P(None, None, "dp", "tensor", None),
            P("dp"),
        ),
        out_specs=(P(None, None, "tensor"), P(None, None, "tensor"), P(None, None, "dp", "tensor")),
        check_vma=False,
    )
```

```python
import jax
import jax.numpy as jnp
from jax import lax
from jax.experimental import pallas as pl
from jax.experimental.pallas import tpu as pltpu
from jax.sharding import PartitionSpec as P

D = 14848
R = 64
ROWS = 8
TAIL = D // 8 % 128
VMEM_BYTES = 32 * 1024 * 1024

rate_a = 0.5
rate_b = 0.05

f32 = jnp.float32
bf16 = jnp.bfloat16


def pick(array, index, axis=0):
    return lax.dynamic_index_in_dim(array, index, axis, keepdims=False)


def split3(x):
    hi = lax.reduce_precision(x, 8, 7)
    mid = lax.reduce_precision(x - hi, 8, 7)
    lo = lax.reduce_precision(x - hi - mid, 8, 7)
    return hi, mid, lo


def nt_dot(a, b):
    return lax.dot_general(a, b, (((1,), (1,)), ((), ())), preferred_element_type=f32)


def in_hbm(x):
    return pltpu.with_memory_space_constraint(x, pltpu.HBM)


def start_all(copies):
    for copy in copies:
        copy.start()
    return copies


def message_kernel(core, owner, own_a, own_b, far_a, far_b, out, both, sems):
    r = own_a.shape[2]

    def run(sources):
        arriving = start_all(
            [
                pltpu.make_async_copy(
                    source.at[0, core[0]], both.at[pl.ds(half * r, r)], sems.at[half]
                )
                for half, source in enumerate(sources)
            ]
        )
        leaving = []
        for half, copy in enumerate(arriving):
            rows = pl.ds(half * r, r)
            copy.wait()
            leaving += start_all(
                [pltpu.make_async_copy(both.at[rows], out.at[rows], sems.at[2 + half])]
            )
        for copy in leaving:
            copy.wait()

    is_mine = owner[core[0]] % 2 == core[0]

    @pl.when(is_mine)
    def _():
        run((own_a, own_b))

    @pl.when(jnp.logical_not(is_mine))
    def _():
        run((far_a, far_b))


def load_tokens(core, sources, held, sems):
    return start_all(
        [
            pltpu.make_async_copy(source.at[core[0]], held.at[i], sems.at[i])
            for i, source in enumerate(sources)
        ]
    )


def token_advantage(info, tails, count, tokens):
    lanes = tails.shape[1]

    def lane_shifted(x, by):
        return pltpu.roll(x, lanes - by, 1)

    rewards = tails + lane_shifted(tails, count) + lane_shifted(tails, 2 * count)
    groups = lane_shifted(tails, 3 * count)
    row = lax.broadcasted_iota(jnp.int32, tails.shape, 0)
    lane = lax.broadcasted_iota(jnp.int32, tails.shape, 1)
    used = (row % ROWS == 0) & (lane >= TAIL) & (lane < TAIL + count)
    sequence = lax.broadcasted_iota(jnp.int32, (1, tokens), 1) // (tokens // count)
    adv = jnp.zeros(sequence.shape, f32)
    for i in range(count):
        same = used & (groups == info[count + i])
        total = jnp.sum(jnp.where(same, rewards, 0.0), keepdims=True)
        members = jnp.sum(jnp.where(same, 1.0, 0.0), keepdims=True)
        adv = jnp.where(sequence == i, info[i] - total / jnp.maximum(members, 1.0), adv)
    return adv


def project_kernel(
    core, info, factors, act, far_act, cot, far_cot, out, adv, held, part, sems, out_sems
):
    r = factors.shape[0] // 2
    _, width, tokens = held.shape
    arriving = load_tokens(core, (act, far_act, cot, far_cot), held, sems)
    tails = factors[:, width // 128 * 128 :].astype(f32)
    adv[...] = token_advantage(info, tails, info.shape[0] // 2, 2 * tokens)
    leaving = []
    for half in range(2):
        rows = pl.ds(half * r, r)
        factor = factors[half * r : (half + 1) * r, :width]
        for place in range(2):
            arriving[2 * half + place].wait()
            part[rows, place * tokens : (place + 1) * tokens] = jnp.dot(
                factor, held[2 * half + place], preferred_element_type=f32
            ).astype(bf16)
        leaving += start_all(
            [
                pltpu.make_async_copy(part.at[rows], out.at[peer, rows], out_sems.at[half, peer])
                for peer in range(out.shape[0])
            ]
        )
    for copy in leaving:
        copy.wait()


def grad_kernel(core, parts, adv_ref, act, far_act, cot, far_cot, out, held, sems):
    r = parts.shape[1] // 2
    _, width, tokens = held.shape
    arriving = load_tokens(core, (act, far_act, cot, far_cot), held, sems)
    adv = adv_ref[...]
    total = jnp.sum(parts[...].astype(f32), axis=0)
    low = (total[:r] * D**-0.5).astype(bf16).astype(f32)
    low = (low * adv).astype(bf16)
    back = (total[r:] * (adv * R**-0.5)).astype(bf16)
    for half, rank in enumerate((back, low)):
        arriving[2 * half].wait()
        grad = nt_dot(rank[:, :tokens], held[2 * half])
        arriving[2 * half + 1].wait()
        grad += nt_dot(rank[:, tokens:], held[2 * half + 1])
        out[half * r : (half + 1) * r] = grad.astype(bf16)


def update_kernel(chip, arrived, piece, out):
    total = jnp.sum(arrived[...].astype(f32), axis=0)
    step = jnp.where(chip[0] * ROWS < R, rate_a * D**-0.5, rate_b * R**-0.5)
    fresh = (piece[...].astype(f32) - step * total).astype(bf16)
    for peer in range(out.shape[0]):
        out[peer] = fresh


def decode_kernel(core, fresh, dec, far_dec, out):
    steps, rows, width = dec.shape
    mine, other = core[0], 1 - core[0]
    for place, source in ((mine, dec), (other, far_dec)):
        part = nt_dot(fresh[: out.shape[2]], source[...].reshape(steps * rows, width)).astype(bf16)
        for peer in range(out.shape[0]):
            out[peer, place] = part


def attend_kernel(
    core,
    rank_ref,
    fresh,
    far_fresh,
    frozen_ref,
    kv_ref,
    new_ref,
    valid_ref,
    new_a,
    new_b,
    out_ref,
    change,
):
    steps, _, rows, width = frozen_ref.shape
    half = kv_ref.shape[3] // 2
    heads = width // half
    pad = -(-heads // 8) * 8
    layer, block = pl.program_id(0), pl.program_id(1)

    def begin(source):
        new_a[0] = source[:R]
        new_b[0] = source[R:]
        rank = (jnp.sum(rank_ref[:, 0].astype(f32), axis=0) * D**-0.5).astype(bf16)
        change[...] = lax.dot_general(
            rank, source[R:], (((0,), (0,)), ((), ())), preferred_element_type=f32
        ).reshape(change.shape)

    @pl.when((block == 0) & (layer == core[0]))
    def _():
        begin(fresh)

    @pl.when((block == 0) & (layer != core[0]))
    def _():
        begin(far_fresh)

    delta = change[:, pl.ds(block * rows, rows)].reshape(steps * rows, width)
    q = frozen_ref[:, 0].reshape(steps * rows, width).astype(f32) + delta * R**-0.5
    q = q.astype(bf16).astype(f32) * (half**-0.5)
    lane = lax.broadcasted_iota(jnp.int32, (steps * rows, 2 * half), 1)
    pieces = [[jnp.zeros((rows, 2 * half), f32)] * pad for _ in range(steps)]
    for pair in range(heads // 2 + heads % 2):
        x = q[:, 2 * half * pair : 2 * half * (pair + 1)]
        if x.shape[1] < 2 * half:
            x = jnp.concatenate([x, jnp.zeros_like(x)], axis=1)
        for odd in range(2):
            head = 2 * pair + odd
            if head >= heads:
                break
            y = jnp.where(lane < half, pltpu.roll(x, half, 1) if odd else x, 0.0)
            for s in range(steps):
                pieces[s][head] = y[s * rows : (s + 1) * rows]
    query = jnp.transpose(jnp.stack(sum(pieces, [])), (1, 0, 2)).astype(bf16)
    place = lax.broadcasted_iota(jnp.int32, (rows, 16, 2 * half), 1)
    tail = jnp.zeros((rows, 16, 2 * half), f32)
    for t in range(steps):
        tail = jnp.where(place == t, new_ref[t, 0].astype(f32)[:, None, :], tail)
    kv = jnp.concatenate([kv_ref[0], tail.astype(bf16)], axis=1)
    scores = jnp.einsum("bqd,bkd->bqk", query, kv, preferred_element_type=f32)
    weights = []
    for s in range(steps):
        mine = scores[:, pad * s : pad * (s + 1)]
        ok = valid_ref[:, s : s + 1, : kv.shape[1]] > 0
        mine = jnp.where(ok, mine, -jnp.inf)
        e = jnp.exp(mine - jnp.max(mine, axis=2, keepdims=True))
        weights.append((e / jnp.sum(e, axis=2, keepdims=True)).astype(bf16))
    weights = jnp.concatenate(weights, axis=1)
    result = jnp.einsum("bqk,bkd->bqd", weights, kv, preferred_element_type=f32)
    result = jnp.transpose(result, (1, 0, 2))
    low = lax.broadcasted_iota(jnp.int32, (rows, 2 * half), 1) < half
    for s in range(steps):
        for pair in range(heads // 2 + heads % 2):
            head = pad * s + 2 * pair
            even = pltpu.roll(result[head], half, 1)
            at = 2 * half * pair
            if 2 * pair + 1 < heads:
                both = jnp.where(low, even, result[head + 1])
                out_ref[s, 0, :, at : at + 2 * half] = both.astype(bf16)
            else:
                out_ref[s, 0, :, at : at + half] = even[:, :half].astype(bf16)


def attend(core, ranks, fresh, far_fresh, frozen, kv, new_kv, valid, rows=64):
    steps, layers, rows_dev, width = frozen.shape
    slots, lanes = kv.shape[2:]
    factor = jax.ShapeDtypeStruct((layers, R, width), bf16)
    return pl.pallas_call(
        attend_kernel,
        grid_spec=pltpu.PrefetchScalarGridSpec(
            num_scalar_prefetch=1,
            grid=(layers, rows_dev // rows),
            in_specs=[
                pl.BlockSpec((ranks.shape[0], 1) + ranks.shape[2:], lambda l, r, c: (0, l, 0, 0)),
                pl.BlockSpec(fresh.shape, lambda l, r, c: (0, 0)),
                pl.BlockSpec(fresh.shape, lambda l, r, c: (0, 0)),
                pl.BlockSpec((steps, 1, rows, width), lambda l, r, c: (0, l, r, 0)),
                pl.BlockSpec((1, rows, slots, lanes), lambda l, r, c: (l, r, 0, 0)),
                pl.BlockSpec((steps, 1, rows, lanes), lambda l, r, c: (0, l, r, 0)),
                pl.BlockSpec((rows, steps, lanes), lambda l, r, c: (r, 0, 0)),
            ],
            out_specs=[
                pl.BlockSpec((1, R, width), lambda l, r, c: (l, 0, 0)),
                pl.BlockSpec((1, R, width), lambda l, r, c: (l, 0, 0)),
                pl.BlockSpec((steps, 1, rows, width), lambda l, r, c: (0, l, r, 0)),
            ],
            scratch_shapes=[pltpu.VMEM((steps, rows_dev, width), f32)],
        ),
        out_shape=[factor, factor, jax.ShapeDtypeStruct(frozen.shape, bf16)],
        compiler_params=pltpu.CompilerParams(vmem_limit_bytes=VMEM_BYTES),
        name="attend",
    )(core.reshape(1), ranks, fresh, far_fresh, frozen, kv, new_kv, valid)


def local_call(kernel, name, scalars, whole, streamed, out, scratch, by_copy=True, beside=None):
    def block(shape):
        return pl.BlockSpec(shape, lambda i, *_: (0,) * len(shape))

    out_spec = pl.BlockSpec(memory_space=pl.ANY) if by_copy else block(out)
    return pl.pallas_call(
        kernel,
        grid_spec=pltpu.PrefetchScalarGridSpec(
            num_scalar_prefetch=len(scalars),
            grid=(1,),
            in_specs=[block(x.shape) for x in whole]
            + [pl.BlockSpec(memory_space=pl.ANY)] * len(streamed),
            out_specs=(out_spec, block(beside.shape)) if beside else out_spec,
            scratch_shapes=scratch,
        ),
        out_shape=(pltpu.HBM(out, bf16), beside) if beside else pltpu.HBM(out, bf16),
        compiler_params=pltpu.CompilerParams(vmem_limit_bytes=VMEM_BYTES),
        name=name,
    )(*scalars, *whole, *streamed)


def shards(
    activations,
    cotangent,
    rewards,
    group_of,
    layer_owner,
    adapter_a,
    adapter_b,
    frozen_query_part,
    decode_in,
    kv_cache,
    new_kv,
    lengths,
):
    n_dp = lax.axis_size("dp")
    n_tensor = lax.axis_size("tensor")
    chips = n_dp // 2
    index = lax.axis_index("dp")
    core = index % 2
    chip = index // 2
    swap = [(i, i ^ 1) for i in range(n_dp)]
    same_core = [[i for i in range(n_dp) if i % 2 == c] for c in range(2)]
    layers, tokens, width = activations.shape
    completions = rewards.shape[0]
    steps, _, rows_dev, _ = decode_in.shape
    slots, lanes = kv_cache.shape[3:]

    def core_swap(x):
        return lax.ppermute(x, "dp", swap)

    def across_chips(x):
        return lax.all_to_all(x, "dp", 0, 0, axis_index_groups=same_core)

    def across_tensor(x):
        return lax.all_to_all(x, "tensor", 0, 0)

    far_a = core_swap(adapter_a)
    far_b = core_swap(adapter_b)
    scalars = [core.reshape(1)]
    candidate = local_call(
        message_kernel,
        "message",
        scalars + [in_hbm(layer_owner)],
        [],
        [in_hbm(adapter_a), in_hbm(adapter_b), far_a, far_b],
        (2 * R, width),
        [pltpu.VMEM((2 * R, width), bf16), pltpu.SemaphoreType.DMA((4,))],
    )
    rows = ROWS

    message, layer_owner, act_out, cot_out, dec_out, rewards, group_of = lax.optimization_barrier(
        (
            candidate.reshape(chips, rows, width),
            layer_owner,
            activations,
            cotangent,
            decode_in,
            rewards,
            group_of,
        )
    )
    arrived = across_chips(message)
    act = jnp.swapaxes(activations, 1, 2)
    cot = jnp.swapaxes(cotangent, 1, 2)
    own_info = jnp.stack([rewards, group_of.astype(f32)])
    far_info = core_swap(own_info)
    far_act = core_swap(jnp.swapaxes(act_out, 1, 2))
    far_cot = core_swap(jnp.swapaxes(cot_out, 1, 2))
    dec = pick(dec_out, core, 1)
    far_dec = core_swap(pick(dec_out, 1 - core, 1))
    column = jnp.arange(lanes)[None, None, :]
    step_of = jnp.arange(steps)[None, :, None]
    valid = column < lengths[:, None, None]
    valid = valid | ((column >= slots) & (column <= slots + step_of))
    info = jnp.concatenate([own_info, far_info], axis=1)
    packed = jnp.concatenate([*split3(info[0]), info[1]]).astype(bf16)
    tail = jnp.zeros((rows, 64), bf16).at[0, : packed.shape[0]].set(packed)
    owner_chip = pick(layer_owner, core) // 2
    info = info.reshape(-1)
    arrived, owner_chip, tail, info, valid, dec, far_dec, far_act, far_cot = (
        lax.optimization_barrier(
            (arrived, owner_chip, tail, info, valid.astype(f32), dec, far_dec, far_act, far_cot)
        )
    )
    piece = pick(arrived, owner_chip)

    message = jnp.concatenate([piece, tail], axis=1)
    factors = across_chips(jnp.broadcast_to(message, (chips,) + message.shape))
    factors = factors.reshape(chips * rows, -1)

    token_arrays = [act, far_act, in_hbm(cot), far_cot]
    token_scratch = [pltpu.VMEM((4, width, tokens), bf16), pltpu.SemaphoreType.DMA((4,))]
    parts, advantage = local_call(
        project_kernel,
        "project",
        scalars + [info],
        [factors],
        token_arrays,
        (n_tensor, 2 * R, 2 * tokens),
        token_scratch[:1]
        + [pltpu.VMEM((2 * R, 2 * tokens), bf16)]
        + token_scratch[1:]
        + [pltpu.SemaphoreType.DMA((2, n_tensor))],
        beside=jax.ShapeDtypeStruct((1, 2 * tokens), f32),
    )
    parts = across_tensor(parts)
    grads = local_call(
        grad_kernel,
        "grads",
        scalars,
        [parts, advantage],
        token_arrays,
        (2 * R, width),
        token_scratch,
        by_copy=False,
    )
    arrived = across_chips(grads.reshape(chips, rows, width))
    fresh = local_call(
        update_kernel,
        "update",
        [chip.reshape(1)],
        [arrived, piece],
        [],
        (chips, rows, width),
        [],
        by_copy=False,
    )
    fresh = across_chips(fresh)
    fresh = fresh.reshape(chips * rows, width)

    ranks = local_call(
        decode_kernel,
        "decode_rank",
        scalars,
        [fresh, dec, far_dec],
        [],
        (n_tensor, 2, R, steps * rows_dev),
        [],
        by_copy=False,
    )
    far_fresh = core_swap(fresh)
    ranks = lax.all_to_all(
        ranks.reshape(n_tensor * 2, R, steps * rows_dev),
        ("dp", "tensor"),
        0,
        0,
        axis_index_groups=[
            [(pair * 2 + c) * n_tensor + t for t in range(n_tensor) for c in range(2)]
            for pair in range(chips)
        ],
    ).reshape(n_tensor, 2, R, steps * rows_dev)

    return attend(
        core,
        ranks,
        fresh,
        far_fresh,
        in_hbm(frozen_query_part),
        in_hbm(kv_cache.reshape(layers, rows_dev, slots, lanes)),
        new_kv.reshape(steps, layers, rows_dev, lanes),
        valid,
    )


def solution(mesh):
    return jax.shard_map(
        shards,
        mesh=mesh,
        in_specs=(
            P(None, "dp", "tensor"),
            P(None, "dp", "tensor"),
            P("dp"),
            P("dp"),
            P(),
            P("dp", None, None, "tensor"),
            P("dp", None, None, "tensor"),
            P(None, None, "dp", "tensor"),
            P(None, None, "dp", "tensor"),
            P(None, "dp", "tensor", None, None),
            P(None, None, "dp", "tensor", None),
            P("dp"),
        ),
        out_specs=(P(None, None, "tensor"), P(None, None, "tensor"), P(None, None, "dp", "tensor")),
        check_vma=False,
    )
```

```python
import jax
import jax.numpy as jnp
from jax import lax
from jax.experimental import pallas as pl
from jax.experimental.pallas import tpu as pltpu
from jax.sharding import PartitionSpec as P

D = 14848
R = 64
ROWS = 8
TAIL = D // 8 % 128
VMEM_BYTES = 32 * 1024 * 1024

rate_a = 0.5
rate_b = 0.05

f32 = jnp.float32
bf16 = jnp.bfloat16


def pick(array, index, axis=0):
    return lax.dynamic_index_in_dim(array, index, axis, keepdims=False)


def split3(x):
    hi = lax.reduce_precision(x, 8, 7)
    mid = lax.reduce_precision(x - hi, 8, 7)
    lo = lax.reduce_precision(x - hi - mid, 8, 7)
    return hi, mid, lo


def nt_dot(a, b):
    return lax.dot_general(a, b, (((1,), (1,)), ((), ())), preferred_element_type=f32)


def in_hbm(x):
    return pltpu.with_memory_space_constraint(x, pltpu.HBM)


def start_all(copies):
    for copy in copies:
        copy.start()
    return copies


def message_kernel(core, owner, own_a, own_b, far_a, far_b, out, both, sems):
    r = own_a.shape[2]

    def run(sources):
        arriving = start_all(
            [
                pltpu.make_async_copy(
                    source.at[0, core[0]], both.at[pl.ds(half * r, r)], sems.at[half]
                )
                for half, source in enumerate(sources)
            ]
        )
        leaving = []
        for half, copy in enumerate(arriving):
            rows = pl.ds(half * r, r)
            copy.wait()
            leaving += start_all(
                [pltpu.make_async_copy(both.at[rows], out.at[rows], sems.at[2 + half])]
            )
        for copy in leaving:
            copy.wait()

    is_mine = owner[core[0]] % 2 == core[0]

    @pl.when(is_mine)
    def _():
        run((own_a, own_b))

    @pl.when(jnp.logical_not(is_mine))
    def _():
        run((far_a, far_b))


def load_tokens(core, sources, held, sems):
    return start_all(
        [
            pltpu.make_async_copy(source.at[core[0]], held.at[i], sems.at[i])
            for i, source in enumerate(sources)
        ]
    )


def token_advantage(info, tails, count, tokens):
    lanes = tails.shape[1]

    def lane_shifted(x, by):
        return pltpu.roll(x, lanes - by, 1)

    rewards = tails + lane_shifted(tails, count) + lane_shifted(tails, 2 * count)
    groups = lane_shifted(tails, 3 * count)
    row = lax.broadcasted_iota(jnp.int32, tails.shape, 0)
    lane = lax.broadcasted_iota(jnp.int32, tails.shape, 1)
    used = (row % ROWS == 0) & (lane >= TAIL) & (lane < TAIL + count)
    sequence = lax.broadcasted_iota(jnp.int32, (1, tokens), 1) // (tokens // count)
    adv = jnp.zeros(sequence.shape, f32)
    for i in range(count):
        same = used & (groups == info[count + i])
        total = jnp.sum(jnp.where(same, rewards, 0.0), keepdims=True)
        members = jnp.sum(jnp.where(same, 1.0, 0.0), keepdims=True)
        adv = jnp.where(sequence == i, info[i] - total / jnp.maximum(members, 1.0), adv)
    return adv


def project_kernel(
    core, info, factors, act, far_act, cot, far_cot, out, adv, held, part, sems, out_sems
):
    r = factors.shape[0] // 2
    _, width, tokens = held.shape
    arriving = load_tokens(core, (act, far_act, cot, far_cot), held, sems)
    tails = factors[:, width // 128 * 128 :].astype(f32)
    adv[...] = token_advantage(info, tails, info.shape[0] // 2, 2 * tokens)
    leaving = []
    for half in range(2):
        rows = pl.ds(half * r, r)
        factor = factors[half * r : (half + 1) * r, :width]
        for place in range(2):
            arriving[2 * half + place].wait()
            part[rows, place * tokens : (place + 1) * tokens] = jnp.dot(
                factor, held[2 * half + place], preferred_element_type=f32
            ).astype(bf16)
        leaving += start_all(
            [
                pltpu.make_async_copy(part.at[rows], out.at[peer, rows], out_sems.at[half, peer])
                for peer in range(out.shape[0])
            ]
        )
    for copy in leaving:
        copy.wait()


def grad_kernel(core, parts, adv_ref, act, far_act, cot, far_cot, out, held, sems):
    r = parts.shape[1] // 2
    _, width, tokens = held.shape
    arriving = load_tokens(core, (act, far_act, cot, far_cot), held, sems)
    adv = adv_ref[...]
    total = jnp.sum(parts[...].astype(f32), axis=0)
    low = (total[:r] * D**-0.5).astype(bf16).astype(f32)
    low = (low * adv).astype(bf16)
    back = (total[r:] * (adv * R**-0.5)).astype(bf16)
    for half, rank in enumerate((back, low)):
        arriving[2 * half].wait()
        grad = nt_dot(rank[:, :tokens], held[2 * half])
        arriving[2 * half + 1].wait()
        grad += nt_dot(rank[:, tokens:], held[2 * half + 1])
        out[half * r : (half + 1) * r] = grad.astype(bf16)


def update_kernel(chip, arrived, piece, out):
    total = jnp.sum(arrived[...].astype(f32), axis=0)
    step = jnp.where(chip[0] * ROWS < R, rate_a * D**-0.5, rate_b * R**-0.5)
    fresh = (piece[...].astype(f32) - step * total).astype(bf16)
    for peer in range(out.shape[0]):
        out[peer] = fresh


def decode_kernel(core, fresh, dec, far_dec, out):
    steps, rows, width = dec.shape
    mine, other = core[0], 1 - core[0]
    for place, source in ((mine, dec), (other, far_dec)):
        part = nt_dot(fresh[: out.shape[2]], source[...].reshape(steps * rows, width)).astype(bf16)
        for peer in range(out.shape[0]):
            out[peer, place] = part


def attend_kernel(
    core,
    rank_ref,
    fresh,
    far_fresh,
    frozen_ref,
    kv_ref,
    new_ref,
    valid_ref,
    new_a,
    new_b,
    out_ref,
    change,
):
    steps, _, rows, width = frozen_ref.shape
    half = kv_ref.shape[3] // 2
    heads = width // half
    pad = -(-heads // 8) * 8
    layer, block = pl.program_id(0), pl.program_id(1)

    def begin(source):
        new_a[0] = source[:R]
        new_b[0] = source[R:]
        rank = (jnp.sum(rank_ref[:, 0].astype(f32), axis=0) * D**-0.5).astype(bf16)
        change[...] = lax.dot_general(
            rank, source[R:], (((0,), (0,)), ((), ())), preferred_element_type=f32
        ).reshape(change.shape)

    @pl.when((block == 0) & (layer == core[0]))
    def _():
        begin(fresh)

    @pl.when((block == 0) & (layer != core[0]))
    def _():
        begin(far_fresh)

    delta = change[:, pl.ds(block * rows, rows)].reshape(steps * rows, width)
    q = frozen_ref[:, 0].reshape(steps * rows, width).astype(f32) + delta * R**-0.5
    q = q.astype(bf16).astype(f32) * (half**-0.5)
    lane = lax.broadcasted_iota(jnp.int32, (steps * rows, 2 * half), 1)
    pieces = [[jnp.zeros((rows, 2 * half), f32)] * pad for _ in range(steps)]
    for pair in range(heads // 2 + heads % 2):
        x = q[:, 2 * half * pair : 2 * half * (pair + 1)]
        if x.shape[1] < 2 * half:
            x = jnp.concatenate([x, jnp.zeros_like(x)], axis=1)
        for odd in range(2):
            head = 2 * pair + odd
            if head >= heads:
                break
            y = jnp.where(lane < half, pltpu.roll(x, half, 1) if odd else x, 0.0)
            for s in range(steps):
                pieces[s][head] = y[s * rows : (s + 1) * rows]
    query = jnp.transpose(jnp.stack(sum(pieces, [])), (1, 0, 2)).astype(bf16)
    place = lax.broadcasted_iota(jnp.int32, (rows, 16, 2 * half), 1)
    tail = jnp.zeros((rows, 16, 2 * half), f32)
    for t in range(steps):
        tail = jnp.where(place == t, new_ref[t, 0].astype(f32)[:, None, :], tail)
    kv = jnp.concatenate([kv_ref[0], tail.astype(bf16)], axis=1)
    scores = jnp.einsum("bqd,bkd->bqk", query, kv, preferred_element_type=f32)
    weights = []
    for s in range(steps):
        mine = scores[:, pad * s : pad * (s + 1)]
        ok = valid_ref[:, s : s + 1, : kv.shape[1]] > 0
        mine = jnp.where(ok, mine, -jnp.inf)
        e = jnp.exp(mine - jnp.max(mine, axis=2, keepdims=True))
        weights.append((e / jnp.sum(e, axis=2, keepdims=True)).astype(bf16))
    weights = jnp.concatenate(weights, axis=1)
    result = jnp.einsum("bqk,bkd->bqd", weights, kv, preferred_element_type=f32)
    result = jnp.transpose(result, (1, 0, 2))
    low = lax.broadcasted_iota(jnp.int32, (rows, 2 * half), 1) < half
    for s in range(steps):
        for pair in range(heads // 2 + heads % 2):
            head = pad * s + 2 * pair
            even = pltpu.roll(result[head], half, 1)
            at = 2 * half * pair
            if 2 * pair + 1 < heads:
                both = jnp.where(low, even, result[head + 1])
                out_ref[s, 0, :, at : at + 2 * half] = both.astype(bf16)
            else:
                out_ref[s, 0, :, at : at + half] = even[:, :half].astype(bf16)


def attend(core, ranks, fresh, far_fresh, frozen, kv, new_kv, valid, rows=64):
    steps, layers, rows_dev, width = frozen.shape
    slots, lanes = kv.shape[2:]
    factor = jax.ShapeDtypeStruct((layers, R, width), bf16)
    return pl.pallas_call(
        attend_kernel,
        grid_spec=pltpu.PrefetchScalarGridSpec(
            num_scalar_prefetch=1,
            grid=(layers, rows_dev // rows),
            in_specs=[
                pl.BlockSpec((ranks.shape[0], 1) + ranks.shape[2:], lambda l, r, c: (0, l, 0, 0)),
                pl.BlockSpec(fresh.shape, lambda l, r, c: (0, 0)),
                pl.BlockSpec(fresh.shape, lambda l, r, c: (0, 0)),
                pl.BlockSpec((steps, 1, rows, width), lambda l, r, c: (0, l, r, 0)),
                pl.BlockSpec((1, rows, slots, lanes), lambda l, r, c: (l, r, 0, 0)),
                pl.BlockSpec((steps, 1, rows, lanes), lambda l, r, c: (0, l, r, 0)),
                pl.BlockSpec((rows, steps, lanes), lambda l, r, c: (r, 0, 0)),
            ],
            out_specs=[
                pl.BlockSpec((1, R, width), lambda l, r, c: (l, 0, 0)),
                pl.BlockSpec((1, R, width), lambda l, r, c: (l, 0, 0)),
                pl.BlockSpec((steps, 1, rows, width), lambda l, r, c: (0, l, r, 0)),
            ],
            scratch_shapes=[pltpu.VMEM((steps, rows_dev, width), f32)],
        ),
        out_shape=[factor, factor, jax.ShapeDtypeStruct(frozen.shape, bf16)],
        compiler_params=pltpu.CompilerParams(vmem_limit_bytes=VMEM_BYTES),
        name="attend",
    )(core.reshape(1), ranks, fresh, far_fresh, frozen, kv, new_kv, valid)


def local_call(kernel, name, scalars, whole, streamed, out, scratch, by_copy=True, beside=None):
    def block(shape):
        return pl.BlockSpec(shape, lambda i, *_: (0,) * len(shape))

    out_spec = pl.BlockSpec(memory_space=pl.ANY) if by_copy else block(out)
    return pl.pallas_call(
        kernel,
        grid_spec=pltpu.PrefetchScalarGridSpec(
            num_scalar_prefetch=len(scalars),
            grid=(1,),
            in_specs=[block(x.shape) for x in whole]
            + [pl.BlockSpec(memory_space=pl.ANY)] * len(streamed),
            out_specs=(out_spec, block(beside.shape)) if beside else out_spec,
            scratch_shapes=scratch,
        ),
        out_shape=(pltpu.HBM(out, bf16), beside) if beside else pltpu.HBM(out, bf16),
        compiler_params=pltpu.CompilerParams(vmem_limit_bytes=VMEM_BYTES),
        name=name,
    )(*scalars, *whole, *streamed)


def shards(
    activations,
    cotangent,
    rewards,
    group_of,
    layer_owner,
    adapter_a,
    adapter_b,
    frozen_query_part,
    decode_in,
    kv_cache,
    new_kv,
    lengths,
):
    n_dp = lax.axis_size("dp")
    n_tensor = lax.axis_size("tensor")
    chips = n_dp // 2
    index = lax.axis_index("dp")
    core = index % 2
    chip = index // 2
    swap = [(i, i ^ 1) for i in range(n_dp)]
    same_core = [[i for i in range(n_dp) if i % 2 == c] for c in range(2)]
    layers, tokens, width = activations.shape
    completions = rewards.shape[0]
    steps, _, rows_dev, _ = decode_in.shape
    slots, lanes = kv_cache.shape[3:]

    def core_swap(x):
        return lax.ppermute(x, "dp", swap)

    def across_chips(x):
        return lax.all_to_all(x, "dp", 0, 0, axis_index_groups=same_core)

    def across_tensor(x):
        return lax.all_to_all(x, "tensor", 0, 0)

    far_a = core_swap(adapter_a)
    far_b = core_swap(adapter_b)
    scalars = [core.reshape(1)]
    candidate = local_call(
        message_kernel,
        "message",
        scalars + [in_hbm(layer_owner)],
        [],
        [in_hbm(adapter_a), in_hbm(adapter_b), far_a, far_b],
        (2 * R, width),
        [pltpu.VMEM((2 * R, width), bf16), pltpu.SemaphoreType.DMA((4,))],
    )
    rows = ROWS

    message, layer_owner, act_out, cot_out, dec_out, rewards, group_of = lax.optimization_barrier(
        (
            candidate.reshape(chips, rows, width),
            layer_owner,
            activations,
            cotangent,
            decode_in,
            rewards,
            group_of,
        )
    )
    arrived = across_chips(message)
    act = jnp.swapaxes(activations, 1, 2)
    cot = jnp.swapaxes(cotangent, 1, 2)
    own_info = jnp.stack([rewards, group_of.astype(f32)])
    far_info = core_swap(own_info)
    far_act = core_swap(jnp.swapaxes(act_out, 1, 2))
    far_cot = core_swap(jnp.swapaxes(cot_out, 1, 2))
    dec = pick(dec_out, core, 1)
    far_dec = core_swap(pick(dec_out, 1 - core, 1))
    column = jnp.arange(lanes)[None, None, :]
    step_of = jnp.arange(steps)[None, :, None]
    valid = column < lengths[:, None, None]
    valid = valid | ((column >= slots) & (column <= slots + step_of))
    info = jnp.concatenate([own_info, far_info], axis=1)
    packed = jnp.concatenate([*split3(info[0]), info[1]]).astype(bf16)
    tail = jnp.zeros((rows, 64), bf16).at[0, : packed.shape[0]].set(packed)
    owner_chip = pick(layer_owner, core) // 2
    info = info.reshape(-1)
    arrived, owner_chip, tail, info, valid, dec, far_dec = lax.optimization_barrier(
        (arrived, owner_chip, tail, info, valid.astype(f32), dec, far_dec)
    )
    piece = pick(arrived, owner_chip)

    message = jnp.concatenate([piece, tail], axis=1)
    factors = across_chips(jnp.broadcast_to(message, (chips,) + message.shape))
    factors = factors.reshape(chips * rows, -1)

    token_arrays = [act, far_act, in_hbm(cot), far_cot]
    token_scratch = [pltpu.VMEM((4, width, tokens), bf16), pltpu.SemaphoreType.DMA((4,))]
    parts, advantage = local_call(
        project_kernel,
        "project",
        scalars + [info],
        [factors],
        token_arrays,
        (n_tensor, 2 * R, 2 * tokens),
        token_scratch[:1]
        + [pltpu.VMEM((2 * R, 2 * tokens), bf16)]
        + token_scratch[1:]
        + [pltpu.SemaphoreType.DMA((2, n_tensor))],
        beside=jax.ShapeDtypeStruct((1, 2 * tokens), f32),
    )
    parts = across_tensor(parts)
    grads = local_call(
        grad_kernel,
        "grads",
        scalars,
        [parts, advantage],
        token_arrays,
        (2 * R, width),
        token_scratch,
        by_copy=False,
    )
    arrived = across_chips(grads.reshape(chips, rows, width))
    fresh = local_call(
        update_kernel,
        "update",
        [chip.reshape(1)],
        [arrived, piece],
        [],
        (chips, rows, width),
        [],
        by_copy=False,
    )
    fresh = across_chips(fresh)
    fresh = fresh.reshape(chips * rows, width)

    ranks = local_call(
        decode_kernel,
        "decode_rank",
        scalars,
        [fresh, dec, far_dec],
        [],
        (n_tensor, 2, R, steps * rows_dev),
        [],
        by_copy=False,
    )
    far_fresh = core_swap(fresh)
    ranks = lax.all_to_all(
        ranks.reshape(n_tensor * 2, R, steps * rows_dev),
        ("dp", "tensor"),
        0,
        0,
        axis_index_groups=[
            [(pair * 2 + c) * n_tensor + t for t in range(n_tensor) for c in range(2)]
            for pair in range(chips)
        ],
    ).reshape(n_tensor, 2, R, steps * rows_dev)

    return attend(
        core,
        ranks,
        fresh,
        far_fresh,
        in_hbm(frozen_query_part),
        in_hbm(kv_cache.reshape(layers, rows_dev, slots, lanes)),
        new_kv.reshape(steps, layers, rows_dev, lanes),
        valid,
    )


def solution(mesh):
    return jax.shard_map(
        shards,
        mesh=mesh,
        in_specs=(
            P(None, "dp", "tensor"),
            P(None, "dp", "tensor"),
            P("dp"),
            P("dp"),
            P(),
            P("dp", None, None, "tensor"),
            P("dp", None, None, "tensor"),
            P(None, None, "dp", "tensor"),
            P(None, None, "dp", "tensor"),
            P(None, "dp", "tensor", None, None),
            P(None, None, "dp", "tensor", None),
            P("dp"),
        ),
        out_specs=(P(None, None, "tensor"), P(None, None, "tensor"), P(None, None, "dp", "tensor")),
        check_vma=False,
    )
```
